32 devices in a mesh: ctx: 8 (over z, y), ch: 4 (over x, core).
Axes of the slice: x: 2, y: 2, z: 4, core: 2. Of those that a mesh axis runs over, the one named last changes fastest.
Arguments:
- gate_medium: bfloat16 [2048, 8192], P('ctx', 'ch'), may hold values from -6 to 6
- key_medium: bfloat16 [2048, 8192], P('ctx', 'ch'), may hold values from -6 to 6
- value_medium: bfloat16 [2048, 8192], P('ctx', 'ch'), may hold values from -16 to 16
- short_medium: float32 [3, 3, 8192], P(None, None, 'ch'), may hold values from -3.5 to 3.5
- filter_medium: float32 [128, 8192], P(None, 'ch'), may hold values from -2 to 2
- skip_medium: float32 [8192], P('ch'), may hold values from -4 to 4
- norm_gain: float32 [8192], P('ch'), may hold values from 0.5 to 1.5
- gate_long: bfloat16 [2048, 8192], P('ctx', 'ch'), may hold values from -6 to 6
- key_long: bfloat16 [2048, 8192], P('ctx', 'ch'), may hold values from -6 to 6
- short_long: float32 [3, 3, 8192], P(None, None, 'ch'), may hold values from -3.5 to 3.5
- decay_rates: float32 [16, 8192], P(None, 'ch'), may hold values from 4.8828125e-06 to 0.0625
- residues: float32 [16, 8192], P(None, 'ch'), may hold values from -1.5 to 1.5
- skip_long: float32 [8192], P('ch'), may hold values from -4 to 4
Outputs:
- mixed_medium: bfloat16 [2048, 8192], P('ctx', 'ch')
- mixed_long: bfloat16 [2048, 8192], P('ctx', 'ch')
The draws below stay inside these ranges and needn't reach their ends.
All inputs are finite; a program needn't handle non-finite values.
Results may differ from the reference program's by a relative error of at most 0.0095.
Values may be sent and summed in bfloat16 or wider, within the bound.
No kernel may reach another device: no remote copies, remote signals or barrier semaphores. Data moves between devices by JAX's collectives and lax.ppermute only.
A program may use at most 64 MiB of HBM per device.

```python
import math
import jax
import jax.numpy as jnp
from jax import lax

D = 8192
TAPS_MR = 128
MODES = 16
TOKENS = 2048


def draw_value_medium(key, part):
    first, second = jax.random.split(key)
    base = jnp.clip(jax.random.normal(first, (TOKENS, D), jnp.float32), -4.0, 4.0)
    spread = jax.random.uniform(second, (TOKENS, 1), jnp.float32, -0.5, 0.5)
    return (base * jnp.power(10.0, spread)).astype(jnp.bfloat16)


def draw_filter_medium(key, part):
    first, second = jax.random.split(key)
    column = jnp.arange(D).astype(jnp.float32) / D
    level = jax.random.uniform(second, (1, D), jnp.float32)
    base = jnp.clip(jax.random.normal(first, (TAPS_MR, D), jnp.float32), -4.0, 4.0)
    rise = jnp.power(3.0, column - 0.5)
    return base * rise[None, :] * jnp.power(10.0, level - 0.5) / math.sqrt(TAPS_MR)


def draw_decay_rates(key, part):
    first = jax.random.fold_in(key, 0)
    lowest = math.log(0.01 / TOKENS)
    highest = math.log(0.0625)
    level = jax.random.uniform(first, (MODES, D), jnp.float32)
    logs = lowest + level * (highest - lowest)
    return jnp.clip(jnp.exp(logs), 0.01 / TOKENS, 0.0625)


def block_scale(key, dims, cuts, low, top_value):
    def one(axis_at, parts):
        heights = jax.random.uniform(jax.random.fold_in(jax.random.fold_in(key, 6), axis_at), (parts,), jnp.float32, low / len(cuts), top_value / len(cuts))
        return jnp.repeat(jnp.exp(heights), dims[axis_at] // parts).reshape((-1,) + (1,) * (len(dims) - axis_at - 1))

    factor_of = one(*cuts[0])
    for cut in cuts[1:]:
        factor_of = factor_of * one(*cut)
    return factor_of


def noise(rng, shape, scale, bound, cuts=(), held_as=jnp.bfloat16):
    factor_of = block_scale(rng, shape, cuts, -0.22, 0.18) if cuts else 1.0
    values = jax.random.normal(rng, shape, jnp.float32) * scale * factor_of
    return jnp.minimum(jnp.maximum(values, -bound), bound).astype(held_as)


def setup_inputs(seed: int = 0) -> dict:
    key_of = jax.random.split(jax.random.key(seed), 14)
    return {
        "gate_medium": noise(key_of[0], (TOKENS, D), 1.0, 6.0, ((0, 8), (1, 4))),
        "key_medium": noise(key_of[1], (TOKENS, D), 1.0, 6.0, ((0, 8), (1, 4))),
        "value_medium": draw_value_medium(jax.random.fold_in(key_of[13], 71), 0),
        "short_medium": noise(key_of[3], (3, 3, D), 3 ** -0.5, 3.5, ((2, 4),), jnp.float32),
        "filter_medium": draw_filter_medium(jax.random.fold_in(key_of[13], 71), 0),
        "skip_medium": noise(key_of[5], (D,), 1.0, 4.0, ((0, 4),), jnp.float32),
        "norm_gain": jnp.clip(1.0 + 0.1 * jax.random.normal(key_of[6], (D,), jnp.float32), 0.5, 1.5),
        "gate_long": noise(key_of[7], (TOKENS, D), 1.0, 6.0, ((0, 8), (1, 4))),
        "key_long": noise(key_of[8], (TOKENS, D), 1.0, 6.0, ((0, 8), (1, 4))),
        "short_long": noise(key_of[9], (3, 3, D), 3 ** -0.5, 3.5, ((2, 4),), jnp.float32),
        "decay_rates": draw_decay_rates(jax.random.fold_in(key_of[13], 71), 0),
        "residues": noise(key_of[11], (MODES, D), 0.25, 1.5, ((1, 4),), jnp.float32),
        "skip_long": noise(key_of[12], (D,), 1.0, 4.0, ((0, 4),), jnp.float32),
    }


def short_filter(extended, weights):
    return weights[0] * extended[2:] + weights[1] * extended[1:-1] + weights[2] * extended[:-2]

def front_pad(values, count):
    return jnp.pad(values, ((count, 0), (0, 0)))

def split_channels(values, groups):
    shaped = values.reshape(values.shape[:-1] + (groups, values.shape[-1] // groups))
    return jnp.moveaxis(shaped, -2, 0)

def merge_channels(values):
    moved = jnp.moveaxis(values, 0, -2)
    return moved.reshape(moved.shape[:-2] + (moved.shape[-2] * moved.shape[-1],))

def medium_operator(pieces):
    gate_medium, key_medium, value_medium, short_medium, filter_medium, skip_medium = pieces
    tap_count = filter_medium.shape[0]
    filtered_gate = short_filter(front_pad(gate_medium, 2), short_medium[0])
    filtered_key = short_filter(front_pad(key_medium, 2), short_medium[1])
    filtered_value = short_filter(front_pad(value_medium, 2), short_medium[2])
    product = (filtered_key * filtered_value).astype(jnp.bfloat16)
    padded = front_pad(product, tap_count - 1)

    def add_tap(offset, total):
        start = jnp.asarray(tap_count - 1 - offset).astype(jnp.int32)
        piece = lax.dynamic_slice_in_dim(padded, start, TOKENS, 0)
        weight = lax.dynamic_index_in_dim(filter_medium, jnp.asarray(offset).astype(jnp.int32), 0, keepdims=False)
        return total + weight * piece
    conv = lax.fori_loop(0, tap_count, add_tap, jnp.zeros(product.shape, jnp.float32))
    conv = conv + skip_medium * product
    return (filtered_gate * conv).astype(jnp.bfloat16)

def long_operator(pieces):
    gate_long, key_long, normed, short_long, decay_rates, residues, skip_long = pieces
    block_rows = 64
    block_count = TOKENS // block_rows
    width = gate_long.shape[1]
    filtered_gate = short_filter(front_pad(gate_long, 2), short_long[0])
    filtered_key = short_filter(front_pad(key_long, 2), short_long[1])
    filtered_value = short_filter(front_pad(normed, 2), short_long[2])
    product = (filtered_key * filtered_value).astype(jnp.bfloat16)
    positions = jnp.arange(block_rows).astype(jnp.float32)
    mode_weight = residues * jnp.sqrt(-jnp.expm1(-2.0 * decay_rates))
    rates_wide = decay_rates[:, None, :]
    to_end = jnp.exp(-rates_wide * (block_rows - 1.0 - positions)[None, :, None])
    from_start = mode_weight[:, None, :] * jnp.exp(-rates_wide * (positions + 1.0)[None, :, None])
    impulse = lax.optimization_barrier(jnp.sum(mode_weight[:, None, :] * jnp.exp(-rates_wide * positions[None, :, None]), axis=0))
    blocks = product.reshape(block_count, block_rows, width)
    padded = jnp.pad(blocks, ((0, 0), (block_rows - 1, 0), (0, 0)))

    def add_tap(offset, total):
        start = jnp.asarray(block_rows - 1 - offset).astype(jnp.int32)
        piece = lax.dynamic_slice_in_dim(padded, start, block_rows, 1)
        weight = lax.dynamic_index_in_dim(impulse, jnp.asarray(offset).astype(jnp.int32), 0, keepdims=False)
        return total + weight * piece
    inner = lax.fori_loop(0, block_rows, add_tap, jnp.zeros(blocks.shape, jnp.float32))
    ends = jnp.einsum('bsc,msc->bmc', blocks.astype(jnp.float32), to_end, precision=lax.Precision.HIGHEST)
    block_decay = jnp.exp(-decay_rates * block_rows)

    def advance(state, end):
        return (block_decay * state + end, state)
    final_state, starts = lax.scan(advance, jnp.zeros(decay_rates.shape, jnp.float32), ends)
    outer = jnp.einsum('bmc,msc->bsc', starts, from_start, precision=lax.Precision.HIGHEST)
    conv = (inner + outer).reshape(TOKENS, width) + skip_long * product
    return (filtered_gate * conv).astype(jnp.bfloat16)

def reference(gate_medium, key_medium, value_medium, short_medium, filter_medium, skip_medium, norm_gain, gate_long, key_long, short_long, decay_rates, residues, skip_long):
    groups = D // 1024 if D % 1024 == 0 else 1
    medium_parts = lax.map(medium_operator, (split_channels(gate_medium, groups), split_channels(key_medium, groups), split_channels(value_medium, groups), split_channels(short_medium, groups), split_channels(filter_medium, groups), split_channels(skip_medium, groups)))
    mixed_medium = merge_channels(medium_parts)
    mean_square = lax.optimization_barrier(jnp.mean(jnp.square(mixed_medium.astype(jnp.float32)), axis=1))
    normed = (mixed_medium * norm_gain * lax.rsqrt(mean_square + 1e-06)[:, None]).astype(jnp.bfloat16)
    long_parts = lax.map(long_operator, (split_channels(gate_long, groups), split_channels(key_long, groups), split_channels(normed, groups), split_channels(short_long, groups), split_channels(decay_rates, groups), split_channels(residues, groups), split_channels(skip_long, groups)))
    mixed_long = merge_channels(long_parts)
    return (mixed_medium, mixed_long)
```

```python
import functools

import jax
import jax.numpy as jnp
import ml_dtypes
import numpy as np
from jax import lax
from jax.experimental import pallas as pl
from jax.experimental.pallas import tpu as pltpu
from jax.sharding import PartitionSpec as P

F32 = jnp.float32
BF16 = jnp.bfloat16
BLOCK = 128
HALF = BLOCK // 2
TILE = 8
LANES = 128
WIDTH = 256


def split_np(values):
    high = values.astype(ml_dtypes.bfloat16)
    low = (values - high.astype(np.float64)).astype(ml_dtypes.bfloat16)
    return high, low


def transforms():
    order = np.concatenate([np.arange(0, BLOCK, 2), np.arange(1, BLOCK, 2)])
    angle = np.pi * (order[:, None] + 0.5) * np.arange(BLOCK)[None, :] / BLOCK
    forward = np.concatenate([np.cos(angle), -np.sin(angle)], 0)
    high, low = split_np(forward)
    exact_rows = np.concatenate([high, low], 1)
    split_rows = np.concatenate([high, high, low], 1)
    back_high, back_low = split_np(forward.T / BLOCK)
    backward = np.concatenate([back_high, back_high, back_low], 1)
    return exact_rows, split_rows, backward


def reversal():
    flip = np.zeros((2 * BLOCK, BLOCK), np.float32)
    flip[np.arange(BLOCK), BLOCK - 1 - np.arange(BLOCK)] = 1.0
    flip[BLOCK + np.arange(BLOCK - 1), BLOCK - 2 - np.arange(BLOCK - 1)] = 1.0
    return flip


def dot(a, b):
    return jnp.dot(a, b, preferred_element_type=F32)


def split(values):
    high = values.astype(BF16)
    return high, (values - high.astype(F32)).astype(BF16)


def forward_exact(matrix, block):
    return dot(matrix, jnp.concatenate([block, block], 0))


def forward_split(matrix, block):
    high, low = split(block)
    return dot(matrix, jnp.concatenate([high, low, high], 0))


def backward_split(matrix, spectrum):
    high, low = split(spectrum)
    return dot(matrix, jnp.concatenate([high, low, high], 0))


def turned(spectrum):
    even_re, odd_re, even_im, odd_im = (spectrum[i * HALF : (i + 1) * HALF] for i in range(4))
    return jnp.concatenate([-even_im, odd_im, even_re, -odd_re], 0)


def times(a, b):
    a_re, a_im, b_re, b_im = a[:BLOCK], a[BLOCK:], b[:BLOCK], b[BLOCK:]
    return jnp.concatenate([a_re * b_re - a_im * b_im, a_re * b_im + a_im * b_re], 0)


def shifted_filter(frame, weights):
    return (
        weights[0:1] * frame
        + weights[1:2] * pltpu.roll(frame, 1, 0)
        + weights[2:3] * pltpu.roll(frame, 2, 0)
    )


def rows_of(shape):
    return lax.broadcasted_iota(jnp.int32, shape, 0)


def pack_kernel(key_top, key_low, value_top, value_low, gate, gate_long, key_long, short, out):
    key = jnp.concatenate([key_top[...], key_low[...]], 0).astype(F32)
    value = jnp.concatenate([value_top[...], value_low[...]], 0).astype(F32)
    product = shifted_filter(key, short[1]) * shifted_filter(value, short[2])
    row = rows_of((TILE, key.shape[1]))
    key_end, value_end = key[-TILE:], value[-TILE:]
    gate_end = gate[...].astype(F32)[TILE:]
    gate_long_end = gate_long[...].astype(F32)[TILE:]
    key_long_end = key_long[...].astype(F32)[TILE:]
    first = jnp.where(
        row < 2, pltpu.roll(key_end, 2, 0), jnp.where(row < 4, pltpu.roll(value_end, 4, 0), gate_end)
    )
    second = jnp.where(
        row < 2,
        pltpu.roll(gate_long_end, 2, 0),
        jnp.where(
            row < 4,
            pltpu.roll(key_long_end, 4, 0),
            jnp.where(row == 4, pltpu.roll(product[TILE : 2 * TILE], 5, 0), 0.0),
        ),
    )
    out[...] = jnp.concatenate([first, second, product[2 * TILE :]], 0).astype(BF16)


def mode_tables(rates, mode, lanes, offset, sign):
    rate = jnp.broadcast_to(rates[mode : mode + 1, lanes], (TILE, LANES))
    row = rows_of((TILE, LANES)).astype(F32)
    return jnp.exp(-rate * (offset + sign * row)), jnp.exp(-TILE * rate)


def response(starts, steps, count, emit):
    parts = list(starts)
    for i in range(count):
        total = parts[0]
        for part in parts[1:]:
            total = total + part
        emit(i, total)
        if i + 1 < count:
            parts = [part * step for part, step in zip(parts, steps)]


def prepare_kernel(taps, rates, weights, split_rows, flip, taps_hat, taps_flip, long_hat, impulse):
    modes = rates.shape[0]
    rows = impulse.shape[0]
    taps_hat[...] = forward_split(split_rows[...], taps[...])
    taps_flip[...] = jnp.dot(
        flip[...], taps[...], preferred_element_type=F32, precision=lax.Precision.HIGHEST
    )
    for tile in range(WIDTH // LANES):
        lanes = slice(tile * LANES, (tile + 1) * LANES)
        starts, steps = [], []
        for mode in range(modes):
            lead, step = mode_tables(rates, mode, lanes, 0.0, 1.0)
            starts.append(lead * weights[mode : mode + 1, lanes])
            steps.append(step)

        def emit(i, total):
            impulse[i * TILE : (i + 1) * TILE, lanes] = total

        response(starts, steps, rows // TILE, emit)
    for block in range(rows // BLOCK):
        long_hat[block] = forward_split(
            split_rows[...], impulse[block * BLOCK : (block + 1) * BLOCK]
        )
    for block in reversed(range(1, rows // BLOCK)):
        long_hat[block] = long_hat[block] + turned(long_hat[block - 1])


def medium_kernel(
    first, gate, key, value, short, skip, halo, taps_hat, taps_flip, exact_rows, backward,
    mixed, mixed_rim, squares, total,
):
    step = pl.program_id(0)
    rows = gate.shape[0]
    halo_part = jnp.where(first[0] == 1, 0.0, halo[...].astype(F32))
    rim = halo_part[:TILE]
    rim_product = halo_part[2 * TILE :]
    key_frame = jnp.concatenate([pltpu.roll(rim, 6, 0), key[...].astype(F32)], 0)
    value_frame = jnp.concatenate([pltpu.roll(rim, 4, 0), value[...].astype(F32)], 0)
    gate_frame = jnp.concatenate([rim, gate[...].astype(F32)], 0)
    product = (
        (shifted_filter(key_frame, short[1]) * shifted_filter(value_frame, short[2])).astype(BF16)
    )[TILE:]
    gate_feat = shifted_filter(gate_frame, short[0])
    before = forward_exact(exact_rows[...], rim_product.astype(BF16))
    conv = []
    for block in range(rows // BLOCK):
        now = forward_exact(exact_rows[...], product[block * BLOCK : (block + 1) * BLOCK])
        spectrum = times(taps_hat[...], now + turned(before))
        conv.append(backward_split(backward[...], spectrum))
        before = now
    last = jnp.sum(taps_flip[:BLOCK] * rim_product, axis=0, keepdims=True)
    last_tap = taps_flip[0:1]
    last_but_one = (
        jnp.sum(taps_flip[BLOCK:] * rim_product, axis=0, keepdims=True)
        + last_tap * halo_part[TILE + 4 : TILE + 5]
    )
    row = rows_of((TILE, WIDTH))
    rim_conv = jnp.where(row == TILE - 1, last, jnp.where(row == TILE - 2, last_but_one, 0.0))
    conv_frame = jnp.concatenate([rim_conv] + conv, 0)
    product_frame = jnp.concatenate([rim_product[-TILE:], product.astype(F32)], 0)
    mixed_frame = (gate_feat * (conv_frame + skip[...] * product_frame)).astype(BF16)
    mixed[...] = mixed_frame[TILE:]
    kept = mixed_frame.astype(F32)
    mixed_rim[...] = kept[:TILE]
    square = kept * kept
    partial = square[:, :LANES]
    for tile in range(1, WIDTH // LANES):
        partial = partial + square[:, tile * LANES : (tile + 1) * LANES]

    @pl.when(step == 0)
    def _():
        total[...] = partial

    @pl.when(step > 0)
    def _():
        total[...] = total[...] + partial

    @pl.when(step == pl.num_programs(0) - 1)
    def _():
        squares[...] = lax.dot_general(
            jnp.ones((TILE, LANES), F32),
            total[...],
            (((1,), (1,)), ((), ())),
            precision=lax.Precision.HIGHEST,
            preferred_element_type=F32,
        )


def state_kernel(
    first, width, mixed, mixed_rim, squares, gain, key_long, halo, short, rates,
    product_out, state, inverse,
):
    @pl.when(pl.program_id(0) == 0)
    def _():
        total = lax.dot_general(
            squares[...] * (1.0 / TILE),
            jnp.ones((TILE, LANES), F32),
            (((0,), (0,)), ((), ())),
            precision=lax.Precision.HIGHEST,
            preferred_element_type=F32,
        )
        inverse[...] = lax.rsqrt(total / width + 1e-06)

    rows = mixed.shape[0]
    scale = jnp.concatenate([inverse[...]] * (WIDTH // LANES), 1)
    mixed_frame = jnp.concatenate([mixed_rim[...], mixed[...].astype(F32)], 0)
    normed = (mixed_frame * gain[...] * scale).astype(BF16).astype(F32)
    rim = jnp.where(first[0] == 1, 0.0, halo[...].astype(F32))[TILE:]
    key_frame = jnp.concatenate([pltpu.roll(rim, 4, 0), key_long[...].astype(F32)], 0)
    product = (shifted_filter(key_frame, short[1]) * shifted_filter(normed, short[2]))[TILE:]
    rounded = product.astype(BF16)
    product_out[...] = rounded
    values = rounded.astype(F32)
    modes = rates.shape[0]
    row = rows_of((TILE, LANES))
    for tile in range(WIDTH // LANES):
        lanes = slice(tile * LANES, (tile + 1) * LANES)
        tails, steps = [], []
        for mode in range(modes):
            tail, step = mode_tables(rates, mode, lanes, TILE - 1.0, -1.0)
            tails.append(tail)
            steps.append(step)
        parts = [values[:TILE, lanes]] * modes
        for i in range(1, rows // TILE):
            piece = values[i * TILE : (i + 1) * TILE, lanes]
            parts = [part * step + piece for part, step in zip(parts, steps)]
        for mode in range(modes):
            state[mode : mode + 1, lanes] = jnp.sum(parts[mode] * tails[mode], axis=0, keepdims=True)


def local_kernel(product, long_hat, skip, exact_rows, backward, out):
    rows = product.shape[0]
    spectra = []
    for block in range(rows // BLOCK):
        part = slice(block * BLOCK, (block + 1) * BLOCK)
        spectra.append(forward_exact(exact_rows[...], product[part]))
        total = times(long_hat[0], spectra[block])
        for lag in range(1, block + 1):
            total = total + times(long_hat[lag], spectra[block - lag])
        out[part] = backward_split(backward[...], total) + skip[...] * product[part].astype(F32)


def finish_kernel(first, state, rates, weights, local, gate_long, halo, short, out):
    rows = local.shape[0]
    modes = rates.shape[0]
    rim = jnp.where(first[0] == 1, 0.0, halo[...].astype(F32))[TILE:]
    gate_frame = jnp.concatenate([pltpu.roll(rim, 6, 0), gate_long[...].astype(F32)], 0)
    gate_feat = shifted_filter(gate_frame, short[0])[TILE:]
    for tile in range(WIDTH // LANES):
        lanes = slice(tile * LANES, (tile + 1) * LANES)
        starts, steps = [], []
        for mode in range(modes):
            lead, step = mode_tables(rates, mode, lanes, 1.0, 1.0)
            starts.append(
                lead * (weights[mode : mode + 1, lanes] * state[mode : mode + 1, lanes])
            )
            steps.append(step)

        def emit(i, total):
            part = slice(i * TILE, (i + 1) * TILE)
            out[part, lanes] = (gate_feat[part, lanes] * (local[part, lanes] + total)).astype(BF16)

        response(starts, steps, rows // TILE, emit)


def columns(rows, row_block=0):
    return pl.BlockSpec((rows, WIDTH), lambda j: (row_block, j))


def stacked(count, rows):
    return pl.BlockSpec((count, rows, WIDTH), lambda j: (0, 0, j))


def whole(*shape):
    return pl.BlockSpec(shape, lambda j: (0,) * len(shape))


SCALAR = pl.BlockSpec(memory_space=pltpu.SMEM)
PARAMS = pltpu.CompilerParams(
    dimension_semantics=("arbitrary",), vmem_limit_bytes=40 * 1024 * 1024
)


def call(kernel, name, width, in_specs, out_specs, out_shape, scratch=(), flops=0, moved=0):
    return pl.pallas_call(
        kernel,
        grid=(width // WIDTH,),
        in_specs=in_specs,
        out_specs=out_specs,
        out_shape=out_shape,
        scratch_shapes=list(scratch),
        compiler_params=PARAMS,
        name=name,
        cost_estimate=pl.CostEstimate(flops=flops, bytes_accessed=moved, transcendentals=0),
    )


def arr(shape, dtype):
    return jax.ShapeDtypeStruct(shape, dtype)


def exchanged(value, axis, flip):
    count = lax.axis_size(axis)
    return lax.ppermute(value, axis, [(source, source ^ flip) for source in range(count)])


def carried_state(state, rates, row_count):
    count = lax.axis_size("ctx")
    place = lax.axis_index("ctx")
    incoming = jnp.zeros_like(state)
    group = 1
    while group < count:
        radix = 4 if count // group >= 4 else 2
        sent = state.astype(BF16)
        got = {0: state}
        for turn in range(1, radix):
            got[turn] = exchanged(sent, "ctx", turn * group).astype(F32)
        digit = (place // group) % radix
        within = (place % group).astype(F32)
        earlier = jnp.zeros_like(state)
        after = jnp.zeros_like(state)
        for turn in range(radix):
            member = digit ^ turn
            behind = (digit - 1 - member).astype(F32) * group + within
            decay = jnp.exp(-rates * (row_count * jnp.maximum(behind, 0.0)))
            earlier = earlier + jnp.where(member < digit, decay * got[turn], 0.0)
            left = ((radix - 1 - member) * group).astype(F32)
            after = after + jnp.exp(-rates * (row_count * left)) * got[turn]
        incoming = incoming + earlier
        state = after
        group *= radix
    return incoming


def body(
    gate_medium,
    key_medium,
    value_medium,
    short_medium,
    filter_medium,
    skip_medium,
    norm_gain,
    gate_long,
    key_long,
    short_long,
    decay_rates,
    residues,
    skip_long,
):
    gate_medium, key_medium, value_medium, gate_long, key_long, filter_medium = (
        pltpu.with_memory_space_constraint(value, pltpu.HBM)
        for value in (gate_medium, key_medium, value_medium, gate_long, key_long, filter_medium)
    )
    rows, width = gate_medium.shape
    modes = decay_rates.shape[0]
    blocks = rows // BLOCK
    frame = rows + TILE
    pack_rows = BLOCK + 2 * TILE
    all_width = width * lax.axis_size("ch")
    exact_rows, split_rows, backward = (jnp.asarray(m) for m in transforms())
    flip = jnp.asarray(reversal())
    end = rows // (2 * TILE) - 1
    lower, upper = columns(BLOCK, blocks - 1), columns(2 * TILE, end - BLOCK // (2 * TILE))
    last = columns(2 * TILE, end)
    pack = call(
        pack_kernel, "pack", width,
        [upper, lower, upper, lower, last, last, last, stacked(3, 3)],
        columns(pack_rows),
        arr((pack_rows, width), BF16),
        flops=30 * pack_rows * width, moved=6 * pack_rows * width,
    )(key_medium, key_medium, value_medium, value_medium, gate_medium, gate_long, key_long, short_medium)
    count = lax.axis_size("ctx")
    halo = lax.ppermute(pack, "ctx", [(s, (s + 1) % count) for s in range(count)])
    first = (lax.axis_index("ctx") == 0).astype(jnp.int32).reshape(1)

    mode_weight = residues * jnp.sqrt(-jnp.expm1(-2.0 * decay_rates))
    taps_hat, taps_flip, long_hat = call(
        prepare_kernel, "prepare", width,
        [columns(BLOCK), columns(modes), columns(modes), whole(*split_rows.shape), whole(*flip.shape)],
        [columns(2 * BLOCK), columns(2 * BLOCK), stacked(blocks, 2 * BLOCK)],
        [
            arr((2 * BLOCK, width), F32),
            arr((2 * BLOCK, width), F32),
            arr((blocks, 2 * BLOCK, width), F32),
        ],
        [pltpu.VMEM((rows, WIDTH), F32)],
        flops=2000 * rows * width, moved=40 * rows * width,
    )(filter_medium, decay_rates, mode_weight, split_rows, flip)

    mixed_medium, mixed_rim, squares = call(
        medium_kernel, "medium", width,
        [
            SCALAR, columns(rows), columns(rows), columns(rows), stacked(3, 3), columns(1),
            columns(pack_rows), columns(2 * BLOCK), columns(2 * BLOCK),
            whole(*exact_rows.shape), whole(*backward.shape),
        ],
        [columns(rows), columns(TILE), whole(TILE, frame)],
        [arr((rows, width), BF16), arr((TILE, width), F32), arr((TILE, frame), F32)],
        [pltpu.VMEM((frame, LANES), F32)],
        flops=2000 * rows * width, moved=30 * rows * width,
    )(
        first, gate_medium, key_medium, value_medium, short_medium, skip_medium[None], halo,
        taps_hat, taps_flip, exact_rows, backward,
    )

    parts = [exchanged(squares, "ch", turn) for turn in range(1, lax.axis_size("ch"))]
    total_squares = squares
    for part in parts:
        total_squares = total_squares + part

    product_long, state = call(
        functools.partial(lambda width_all, first, *refs: state_kernel(first, width_all, *refs), all_width),
        "state", width,
        [
            SCALAR, columns(rows), columns(TILE), whole(TILE, frame), columns(1), columns(rows),
            columns(2 * TILE), stacked(3, 3), columns(modes),
        ],
        [columns(rows), columns(modes)],
        [arr((rows, width), BF16), arr((modes, width), F32)],
        [pltpu.VMEM((frame, LANES), F32)],
        flops=100 * rows * width, moved=10 * rows * width,
    )(
        first, mixed_medium, mixed_rim, total_squares, norm_gain[None], key_long, halo, short_long,
        decay_rates,
    )

    incoming = carried_state(state, decay_rates, rows)
    local = call(
        local_kernel, "local", width,
        [
            columns(rows), stacked(blocks, 2 * BLOCK), columns(1), whole(*exact_rows.shape),
            whole(*backward.shape),
        ],
        columns(rows),
        arr((rows, width), F32),
        flops=2000 * rows * width, moved=14 * rows * width,
    )(product_long, long_hat, skip_long[None], exact_rows, backward)

    mixed_long = call(
        finish_kernel, "finish", width,
        [
            SCALAR, columns(modes), columns(modes), columns(modes), columns(rows), columns(rows),
            columns(2 * TILE), stacked(3, 3),
        ],
        columns(rows),
        arr((rows, width), BF16),
        flops=100 * rows * width, moved=8 * rows * width,
    )(first, incoming, decay_rates, mode_weight, local, gate_long, halo, short_long)
    return (mixed_medium, mixed_long)


def solution(mesh):
    placed = (
        P("ctx", "ch"),
        P("ctx", "ch"),
        P("ctx", "ch"),
        P(None, None, "ch"),
        P(None, "ch"),
        P("ch"),
        P("ch"),
        P("ctx", "ch"),
        P("ctx", "ch"),
        P(None, None, "ch"),
        P(None, "ch"),
        P(None, "ch"),
        P("ch"),
    )
    return jax.shard_map(
        body,
        mesh=mesh,
        in_specs=placed,
        out_specs=(P("ctx", "ch"), P("ctx", "ch")),
        check_vma=False,
    )
```

```python
import jax
import jax.numpy as jnp
import ml_dtypes
import numpy as np
from jax import lax
from jax.experimental import pallas as pl
from jax.experimental.pallas import tpu as pltpu
from jax.sharding import PartitionSpec as P

F32 = jnp.float32
BF16 = jnp.bfloat16
BLOCK = 128
HALF = BLOCK // 2
TILE = 8
LANES = 128
WIDTH = 1024


RIM = 2 * TILE
EARLY = BLOCK + RIM


def split_np(values):
    high = values.astype(ml_dtypes.bfloat16)
    low = (values - high.astype(np.float64)).astype(ml_dtypes.bfloat16)
    return high, low


def angles(times):
    order = np.concatenate([np.arange(0, BLOCK, 2), np.arange(1, BLOCK, 2)])
    return np.pi * (order[:, None] + 0.5) * times[None, :] / BLOCK


def transforms():
    angle = angles(np.arange(BLOCK))
    forward = np.concatenate([np.cos(angle), -np.sin(angle)], 0)
    high, low = split_np(forward)
    exact_rows = np.concatenate([high, low], 1)
    split_rows = np.concatenate([high, high, low], 1)
    backward = np.concatenate(split_np(forward.T / BLOCK), 0)
    times = np.arange(-RIM, EARLY) + BLOCK - 2
    angle = angles(times)
    late = np.concatenate([np.cos(angle), -np.sin(angle)], 0).T / BLOCK
    late = late * ((times >= BLOCK - 4) & (times < 2 * BLOCK - 1))[:, None]
    return exact_rows, split_rows, backward, np.concatenate(split_np(late), 0)


def dot(a, b):
    return jnp.dot(a, b, preferred_element_type=F32)


def split(values):
    high = values.astype(BF16)
    return high, (values - high.astype(F32)).astype(BF16)


def forward_exact(matrix, block):
    return dot(matrix, jnp.concatenate([block, block], 0))


def forward_split(matrix, block):
    high, low = split(block)
    return dot(matrix, jnp.concatenate([high, low, high], 0))


def backward_split(matrix, spectrum):
    high, low = split(spectrum)
    rows = matrix.shape[0] // 2
    both = dot(matrix, high)
    return both[:rows] + both[rows:] + dot(matrix[:rows], low)


def turned(spectrum):
    even_re, odd_re, even_im, odd_im = (spectrum[i * HALF : (i + 1) * HALF] for i in range(4))
    return jnp.concatenate([-even_im, odd_im, even_re, -odd_re], 0)


def times(a, b):
    a_re, a_im, b_re, b_im = a[:BLOCK], a[BLOCK:], b[:BLOCK], b[BLOCK:]
    return jnp.concatenate([a_re * b_re - a_im * b_im, a_re * b_im + a_im * b_re], 0)


def shifted_filter(frame, weights):
    return (
        weights[0:1] * frame
        + weights[1:2] * pltpu.roll(frame, 1, 0)
        + weights[2:3] * pltpu.roll(frame, 2, 0)
    )


def rows_of(shape):
    return lax.broadcasted_iota(jnp.int32, shape, 0)


def over_channels(width, step):
    def one(i, _):
        step(pl.ds(pl.multiple_of(i * WIDTH, WIDTH), WIDTH), i * WIDTH)
        return 0

    lax.fori_loop(0, width // WIDTH, one, 0)


def sublane_sum(values):
    return jnp.sum(values, axis=0, keepdims=True)


def lane_parts(values):
    total = values[:, :LANES]
    for tile in range(1, values.shape[1] // LANES):
        total = total + values[:, tile * LANES : (tile + 1) * LANES]
    return total


def pack_kernel(key_top, key_low, value_top, value_low, gate, gate_long, key_long, short, out):
    key = jnp.concatenate([key_top[...], key_low[...]], 0).astype(F32)
    value = jnp.concatenate([value_top[...], value_low[...]], 0).astype(F32)
    product = shifted_filter(key, short[1]) * shifted_filter(value, short[2])
    product = pltpu.roll(product, product.shape[0] - 2, 0)
    row = rows_of((TILE, key.shape[1]))
    key_end, value_end = key[-TILE:], value[-TILE:]
    gate_end = gate[...].astype(F32)[TILE:]
    gate_long_end = gate_long[...].astype(F32)[TILE:]
    key_long_end = key_long[...].astype(F32)[TILE:]
    first = jnp.where(
        row < 2, pltpu.roll(key_end, 2, 0), jnp.where(row < 4, pltpu.roll(value_end, 4, 0), gate_end)
    )
    second = jnp.where(
        row < 2,
        pltpu.roll(gate_long_end, 2, 0),
        jnp.where(row < 4, pltpu.roll(key_long_end, 4, 0), product[TILE:RIM]),
    )
    out[...] = jnp.concatenate([first, second, product[RIM:]], 0).astype(BF16)


def mode_tables(rates, mode, lanes, offset, sign):
    rate = jnp.broadcast_to(rates[mode : mode + 1, lanes], (TILE, LANES))
    row = rows_of((TILE, LANES)).astype(F32)
    return jnp.exp(-rate * (offset + sign * row)), jnp.exp(-TILE * rate)


def response(starts, steps, count, emit):
    parts = list(starts)
    for i in range(count):
        level = parts
        while len(level) > 1:
            level = [a + b for a, b in zip(level[::2], level[1::2])]
        emit(i, level[0])
        if i + 1 < count:
            parts = [part * step for part, step in zip(parts, steps)]


def lane_tiles(base):
    return [
        pl.ds(pl.multiple_of(base + tile * LANES, LANES), LANES) for tile in range(WIDTH // LANES)
    ]


def impulse_kernel(count, place, rates, weights, split_rows, long_hat, carry, impulse):
    modes, width = rates.shape
    rows = impulse.shape[0]
    for i, weight in enumerate(carry_weights(place[0], count, rows, rates[...])):
        carry[i] = weight

    def step(here, base):
        for tile, lanes in enumerate(lane_tiles(base)):
            starts, steps = [], []
            for mode in range(modes):
                lead, decay = mode_tables(rates, mode, lanes, 0.0, 1.0)
                starts.append(lead * weights[mode : mode + 1, lanes])
                steps.append(decay)

            def emit(i, total):
                impulse[i * TILE : (i + 1) * TILE, tile * LANES : (tile + 1) * LANES] = total

            response(starts, steps, rows // TILE, emit)
        for block in range(rows // BLOCK):
            long_hat[block, :, here] = forward_split(
                split_rows[...], impulse[block * BLOCK : (block + 1) * BLOCK]
            )
        for block in reversed(range(1, rows // BLOCK)):
            long_hat[block, :, here] = long_hat[block, :, here] + turned(
                long_hat[block - 1, :, here]
            )

    over_channels(width, step)


def own_kernel(
    gate, key, value, key_long, short, short_long, skip, taps, split_rows, exact_rows, backward,
    conv_early, gate_early, mixed_late, squares_late, key_feat, taps_hat, heads,
):
    rows = gate.shape[0]

    @pl.when(pl.program_id(0) == 0)
    def _():
        squares_late[...] = jnp.zeros(squares_late.shape, F32)

    taps_hat[...] = forward_split(split_rows[...], taps[...])
    keys, values, gates = (ref[...].astype(F32) for ref in (key, value, gate))
    keys_long = key_long[...].astype(F32)
    heads[...] = jnp.concatenate(
        [part[:TILE] for part in (keys, values, gates, keys_long)] + [taps[BLOCK - TILE :]], 0
    )
    product = shifted_filter(keys, short[1]) * shifted_filter(values, short[2])
    row = rows_of((TILE, WIDTH))
    product = jnp.concatenate(
        [jnp.where(row < 2, 0.0, product[:TILE]), product[TILE:]], 0
    ).astype(BF16)
    before = None
    conv = []
    for block in range(rows // BLOCK):
        now = forward_exact(exact_rows[...], product[block * BLOCK : (block + 1) * BLOCK])
        window = now if before is None else now + turned(before)
        conv.append(backward_split(backward[...], times(taps_hat[...], window)))
        before = now
    total = jnp.concatenate(conv, 0) + skip[...] * product.astype(F32)
    feat = shifted_filter(gates, short[0])
    conv_early[...] = total[:EARLY]
    gate_early[...] = feat[:EARLY]
    mixed = (feat[EARLY:] * total[EARLY:]).astype(BF16)
    mixed_late[...] = mixed
    kept = mixed.astype(F32)
    squares_late[...] = squares_late[...] + lane_parts(kept * kept)
    key_feat[...] = shifted_filter(keys_long, short_long[1])


def medium_kernel(
    halo, heads, short, skip, taps_hat, exact_rows, backward,
    conv_early, gate_early, mixed_late, squares_late, _,
    mixed, mixed_rim, squares, rim_long, total,
):
    width = halo.shape[1]
    total[...] = jnp.zeros(total.shape, F32)

    def step(here, base):
        halo_part = halo[:, here].astype(F32)
        rim, rim_late = halo_part[:TILE], halo_part[TILE:RIM]
        rim_long[:, here] = rim_late
        row = rows_of((TILE, WIDTH))
        key_part, value_part, gate_part, _, tail = (
            heads[i * TILE : (i + 1) * TILE, here] for i in range(5)
        )
        keys = jnp.where(row >= 6, pltpu.roll(key_part, 6, 0), pltpu.roll(rim, 4, 0))
        values = jnp.where(row >= 6, pltpu.roll(value_part, 6, 0), pltpu.roll(rim, 2, 0))
        start = shifted_filter(keys, short[1, :, here]) * shifted_filter(values, short[2, :, here])
        start = start.astype(BF16).astype(F32)
        end = jnp.where(row >= 6, start, halo_part[-TILE:])
        window = jnp.concatenate([halo_part[RIM:-TILE], end], 0).astype(BF16)
        spectrum = times(taps_hat[:, here], forward_exact(exact_rows[...], window))
        late = backward_split(backward[...], spectrum)
        tap_a, tap_b, tap_c = (tail[i : i + 1] for i in (7, 6, 5))
        far_a, far_b, far_c = (rim_late[i : i + 1] for i in (5, 6, 7))
        skip_part = skip[:, here]
        rim_conv = late[TILE:RIM] + skip_part * pltpu.roll(end, 2, 0)
        rim_conv = rim_conv + jnp.where(
            row == 6, tap_a * far_a + tap_b * far_b + tap_c * far_c, tap_a * far_b + tap_b * far_c
        )
        rim_conv = jnp.where(row >= 6, rim_conv, 0.0)
        early = conv_early[:, here] + late[RIM:]
        extra = skip_part * jnp.where(row < 2, pltpu.roll(start, 2, 0), 0.0)
        extra = extra + jnp.where(row == 0, tap_a * far_c, 0.0)
        gates = shifted_filter(jnp.concatenate([rim, gate_part], 0), short[0, :, here])
        conv = jnp.concatenate([rim_conv, early[:TILE] + extra, early[TILE:]], 0)
        feat = jnp.concatenate([gates, gate_early[TILE:, here]], 0)
        result = (feat * conv).astype(BF16)
        mixed[:EARLY, here] = result[TILE:]
        mixed[EARLY:, here] = mixed_late[:, here]
        kept = result.astype(F32)
        mixed_rim[:, here] = kept[:TILE]
        total[...] = total[...] + lane_parts(kept * kept)

    over_channels(width, step)
    squares[...] = lax.dot_general(
        jnp.ones((TILE, LANES), F32),
        jnp.concatenate([total[...], squares_late[...]], 0),
        (((1,), (1,)), ((), ())),
        precision=lax.Precision.HIGHEST,
        preferred_element_type=F32,
    )


def state_kernel(
    all_width, mixed, mixed_rim, squares, gain, key_feat, heads, rim_long, short, rates,
    product_out, state, inverse,
):
    rows, width = mixed.shape
    modes = rates.shape[0]
    total = lax.dot_general(
        squares[...] * (1.0 / TILE),
        jnp.ones((TILE, LANES), F32),
        (((0,), (0,)), ((), ())),
        precision=lax.Precision.HIGHEST,
        preferred_element_type=F32,
    )
    inverse[...] = lax.rsqrt(total / all_width + 1e-06)

    def step(here, base):
        scale = jnp.concatenate([inverse[...]] * (WIDTH // LANES), 1)
        frame = jnp.concatenate([mixed_rim[:, here], mixed[:, here].astype(F32)], 0) * scale
        feat = shifted_filter(frame, short[2, :, here] * gain[:, here])[TILE:]
        keys = shifted_filter(
            jnp.concatenate(
                [pltpu.roll(rim_long[:, here], 4, 0), heads[3 * TILE : 4 * TILE, here]], 0
            ),
            short[1, :, here],
        )[TILE:]
        keys = jnp.concatenate([keys, key_feat[TILE:, here]], 0)
        rounded = (keys * feat).astype(BF16)
        product_out[:, here] = rounded
        values = rounded.astype(F32)
        for tile, lanes in enumerate(lane_tiles(base)):
            part_lanes = slice(tile * LANES, (tile + 1) * LANES)
            tails, steps = [], []
            for mode in range(modes):
                tail, decay = mode_tables(rates, mode, lanes, TILE - 1.0, -1.0)
                tails.append(tail)
                steps.append(decay)
            parts = [values[:TILE, part_lanes]] * modes
            for i in range(1, rows // TILE):
                piece = values[i * TILE : (i + 1) * TILE, part_lanes]
                parts = [part * decay + piece for part, decay in zip(parts, steps)]
            for mode in range(modes):
                state[mode : mode + 1, lanes] = sublane_sum(parts[mode] * tails[mode])

    over_channels(width, step)


def local_kernel(
    product, long_hat, skip, exact_rows, backward, gate_long, rim_long, short, mixed,
    out, gate_feat, mixed_out, done,
):
    rows, width = product.shape
    done[...] = jnp.zeros(done.shape, F32)

    def step(here, base):
        mixed_out[:, here] = mixed[:, here]
        gates = jnp.concatenate(
            [pltpu.roll(rim_long[:, here], 6, 0), gate_long[:, here].astype(F32)], 0
        )
        feat = shifted_filter(gates, short[0, :, here])[TILE:]
        gate_feat[:, here] = feat
        spectra = []
        for block in range(rows // BLOCK):
            part = slice(block * BLOCK, (block + 1) * BLOCK)
            piece = product[part, here]
            spectra.append(forward_exact(exact_rows[...], piece))
            total = times(long_hat[0, :, here], spectra[block])
            for lag in range(1, block + 1):
                total = total + times(long_hat[lag, :, here], spectra[block - lag])
            conv = backward_split(backward[...], total) + skip[:, here] * piece.astype(F32)
            out[part, here] = feat[part] * conv

    over_channels(width, step)


def finish_kernel(state, rates, weights, local, gate_feat, out):
    rows, width = local.shape
    modes = rates.shape[0]

    def step(here, base):
        for lanes in lane_tiles(base):
            starts, steps = [], []
            for mode in range(modes):
                lead, decay = mode_tables(rates, mode, lanes, 1.0, 1.0)
                starts.append(
                    lead * (weights[mode : mode + 1, lanes] * state[mode : mode + 1, lanes])
                )
                steps.append(decay)
            held = []

            def emit(i, total):
                part = slice(i * TILE, (i + 1) * TILE)
                held.append(local[part, lanes] + gate_feat[part, lanes] * total)
                if i % 2 == 1:
                    out[(i - 1) * TILE : (i + 1) * TILE, lanes] = jnp.concatenate(
                        held[-2:], 0
                    ).astype(BF16)

            response(starts, steps, rows // TILE, emit)

    over_channels(width, step)


def columns(rows, row_block=0):
    return pl.BlockSpec((rows, WIDTH), lambda j: (row_block, j))


def stacked(count, rows):
    return pl.BlockSpec((count, rows, WIDTH), lambda j: (0, 0, j))


def whole(*shape):
    return pl.BlockSpec(shape, lambda j: (0,) * len(shape))


KEPT = pl.BlockSpec(memory_space=pltpu.VMEM)
MIB = 1024 * 1024


def call(kernel, name, in_specs, out_shape, scratch=(), out_specs=None, steps=0, flops=0, moved=0, room=10):
    if out_specs is None:
        out_specs = jax.tree.map(lambda _: KEPT, out_shape)
    return pl.pallas_call(
        kernel,
        grid=(steps,) if steps else (),
        in_specs=in_specs,
        out_specs=out_specs,
        out_shape=out_shape,
        scratch_shapes=list(scratch),
        compiler_params=pltpu.CompilerParams(vmem_limit_bytes=room * MIB),
        name=name,
        cost_estimate=pl.CostEstimate(flops=flops, bytes_accessed=moved, transcendentals=0),
    )


def in_hbm(value):
    return pltpu.with_memory_space_constraint(value, pltpu.HBM)


def arr(shape, dtype):
    return jax.ShapeDtypeStruct(shape, dtype)


def passed_along(value, axis, steps):
    count = lax.axis_size(axis)
    return lax.ppermute(value, axis, [(source, source + steps) for source in range(count - steps)])


def exchanged(value, axis, flip):
    count = lax.axis_size(axis)
    return lax.ppermute(value, axis, [(source, source ^ flip) for source in range(count)])


def stages(count):
    group = 1
    while group < count:
        radix = 4 if count // group >= 4 else 2
        yield group, radix
        group *= radix


def carry_weights(place, count, row_count, rates):
    for group, radix in stages(count):
        digit = (place // group) % radix
        within = (place % group).astype(F32)
        for turn in range(radix):
            member = digit ^ turn
            behind = (digit - 1 - member).astype(F32) * group + within
            decay = jnp.exp(-rates * (row_count * jnp.maximum(behind, 0.0)))
            yield jnp.where(member < digit, decay, 0.0)
            left = ((radix - 1 - member) * group).astype(F32)
            yield jnp.exp(-rates * (row_count * left))


def carried_state(state, weights, beside):
    count = lax.axis_size("ctx")
    incoming = jnp.zeros_like(state)
    at = 0
    for group, radix in stages(count):
        if group > 1 and group * radix == count:
            state = state + beside
        sent = state.astype(BF16)
        got = [state]
        for turn in range(1, radix):
            got.append(exchanged(sent, "ctx", turn * group).astype(F32))
        for turn in range(radix):
            incoming = incoming + weights[at + 2 * turn] * got[turn]
        state = sum(weights[at + 2 * turn + 1] * got[turn] for turn in range(radix))
        at += 2 * radix
    return incoming


def body(
    gate_medium,
    key_medium,
    value_medium,
    short_medium,
    filter_medium,
    skip_medium,
    norm_gain,
    gate_long,
    key_long,
    short_long,
    decay_rates,
    residues,
    skip_long,
):
    rows, width = gate_medium.shape
    modes = decay_rates.shape[0]
    blocks = rows // BLOCK
    frame = rows + TILE
    count = lax.axis_size("ctx")
    all_width = width * lax.axis_size("ch")
    exact_rows, split_rows, backward, backward_late = (jnp.asarray(m) for m in transforms())
    gate_long_kept, short_kept = gate_long, short_medium
    gate_medium, key_medium, value_medium, gate_long, key_long, filter_medium, short_medium = (
        in_hbm(value)
        for value in (
            gate_medium, key_medium, value_medium, gate_long, key_long, filter_medium, short_medium
        )
    )
    steps = width // WIDTH
    end = rows // RIM - 1
    lower, upper = columns(BLOCK, blocks - 1), columns(RIM, end - BLOCK // RIM)
    last = columns(RIM, end)
    pack = call(
        pack_kernel, "pack",
        [upper, lower, upper, lower, last, last, last, stacked(3, 3)],
        arr((EARLY, width), BF16), out_specs=columns(EARLY), steps=steps,
    )(key_medium, key_medium, value_medium, value_medium, gate_medium, gate_long, key_long, short_medium)
    halo = passed_along(pack, "ctx", 1)

    skip_row = skip_medium[None]
    conv_early, gate_early, mixed_late, squares_late, key_feat, taps_hat, heads = call(
        own_kernel, "own",
        [
            columns(rows), columns(rows), columns(rows), columns(rows), stacked(3, 3),
            stacked(3, 3), columns(1), columns(BLOCK), whole(*split_rows.shape),
            whole(*exact_rows.shape), whole(*backward.shape),
        ],
        [
            arr((EARLY, width), F32), arr((EARLY, width), F32),
            arr((rows - EARLY, width), BF16), arr((rows - EARLY, LANES), F32),
            arr((rows, width), F32), arr((2 * BLOCK, width), F32), arr((5 * TILE, width), F32),
        ],
        out_specs=[
            columns(EARLY), columns(EARLY), columns(rows - EARLY), whole(rows - EARLY, LANES),
            columns(rows), columns(2 * BLOCK), columns(5 * TILE),
        ],
        steps=steps, flops=2000 * rows * width, moved=10 * rows * width, room=24,
    )(
        gate_medium, key_medium, value_medium, key_long, short_medium, short_long, skip_row,
        filter_medium, split_rows, exact_rows, backward,
    )

    mode_weight = residues * jnp.sqrt(-jnp.expm1(-2.0 * decay_rates))
    place = lax.axis_index("ctx").astype(jnp.int32).reshape(1)
    turns = sum(2 * radix for _, radix in stages(count))
    long_hat, carry = call(
        lambda *refs: impulse_kernel(count, *refs), "impulse",
        [pl.BlockSpec(memory_space=pltpu.SMEM)] + [KEPT] * 3,
        [arr((blocks, 2 * BLOCK, width), F32), arr((turns, modes, width), F32)],
        [pltpu.VMEM((rows, WIDTH), F32)],
        flops=2000 * rows * width, moved=10 * rows * width,
    )(place, decay_rates, mode_weight, split_rows)

    mixed_medium, mixed_rim, squares, rim_long = call(
        medium_kernel, "medium", [KEPT] * 12,
        [
            arr((rows, width), BF16), arr((TILE, width), F32), arr((TILE, frame), F32),
            arr((TILE, width), F32),
        ],
        [pltpu.VMEM((EARLY + TILE, LANES), F32)],
        flops=1000 * rows * width, moved=10 * rows * width,
    )(
        halo, heads, short_kept, skip_row, taps_hat, exact_rows, backward_late,
        conv_early, gate_early, mixed_late, squares_late, carry,
    )

    parts = [exchanged(squares, "ch", turn) for turn in range(1, lax.axis_size("ch"))]
    total_squares = squares
    for part in parts:
        total_squares = total_squares + part

    product_long, state = call(
        lambda *refs: state_kernel(all_width, *refs), "state", [KEPT] * 9,
        [arr((rows, width), BF16), arr((modes, width), F32)],
        [pltpu.VMEM((frame, LANES), F32)],
        flops=100 * rows * width, moved=10 * rows * width,
    )(
        mixed_medium, mixed_rim, total_squares, norm_gain[None], key_feat, heads, rim_long,
        short_long, decay_rates,
    )

    local, gate_feat, mixed_out, done = call(
        local_kernel, "local", [KEPT] * 9,
        [
            arr((rows, width), F32), arr((rows, width), F32), arr((rows, width), BF16),
            arr((1, width), F32),
        ],
        flops=2000 * rows * width, moved=14 * rows * width,
    )(
        product_long, long_hat, skip_long[None], exact_rows, backward, gate_long_kept, rim_long,
        short_long, mixed_medium,
    )
    incoming = carried_state(state, carry, done)
    mixed_long = call(
        finish_kernel, "finish", [KEPT] * 5, arr((rows, width), BF16),
        flops=100 * rows * width, moved=8 * rows * width,
    )(incoming, decay_rates, mode_weight, local, gate_feat)
    return (mixed_out, mixed_long)


def solution(mesh):
    placed = (
        P("ctx", "ch"),
        P("ctx", "ch"),
        P("ctx", "ch"),
        P(None, None, "ch"),
        P(None, "ch"),
        P("ch"),
        P("ch"),
        P("ctx", "ch"),
        P("ctx", "ch"),
        P(None, None, "ch"),
        P(None, "ch"),
        P(None, "ch"),
        P("ch"),
    )
    return jax.shard_map(
        body,
        mesh=mesh,
        in_specs=placed,
        out_specs=(P("ctx", "ch"), P("ctx", "ch")),
        check_vma=False,
    )
```

```python
import jax
import jax.numpy as jnp
import ml_dtypes
import numpy as np
from jax import lax
from jax.experimental import pallas as pl
from jax.experimental.pallas import tpu as pltpu
from jax.sharding import PartitionSpec as P

F32 = jnp.float32
BF16 = jnp.bfloat16
BLOCK = 128
HALF = BLOCK // 2
TILE = 8
LANES = 128
WIDTH = 1024
PART = 512


RIM = 2 * TILE
EARLY = BLOCK + RIM


def split_np(values):
    high = values.astype(ml_dtypes.bfloat16)
    low = (values - high.astype(np.float64)).astype(ml_dtypes.bfloat16)
    return high, low


def angles(times):
    order = np.concatenate([np.arange(0, BLOCK, 2), np.arange(1, BLOCK, 2)])
    return np.pi * (order[:, None] + 0.5) * times[None, :] / BLOCK


def transforms():
    angle = angles(np.arange(BLOCK))
    forward = np.concatenate([np.cos(angle), -np.sin(angle)], 0)
    high, low = split_np(forward)
    exact_rows = np.concatenate([high, low], 1)
    split_rows = np.concatenate([high, high, low], 1)
    backward = np.concatenate(split_np(forward.T / BLOCK), 0)
    times = np.arange(-RIM, EARLY) + BLOCK - 2
    angle = angles(times)
    late = np.concatenate([np.cos(angle), -np.sin(angle)], 0).T / BLOCK
    late = late * ((times >= BLOCK - 4) & (times < 2 * BLOCK - 1))[:, None]
    return exact_rows, split_rows, backward, np.concatenate(split_np(late), 0)


def dot(a, b):
    return jnp.dot(a, b, preferred_element_type=F32)


def split(values):
    high = values.astype(BF16)
    return high, (values - high.astype(F32)).astype(BF16)


def forward_exact(matrix, block):
    return dot(matrix, jnp.concatenate([block, block], 0))


def forward_split(matrix, block):
    high, low = split(block)
    return dot(matrix, jnp.concatenate([high, low, high], 0))


def backward_exact(matrix, spectrum):
    rows = matrix.shape[0] // 2
    both = dot(matrix, spectrum.astype(BF16))
    return both[:rows] + both[rows:]


def turned(spectrum):
    even_re, odd_re, even_im, odd_im = (spectrum[i * HALF : (i + 1) * HALF] for i in range(4))
    return jnp.concatenate([-even_im, odd_im, even_re, -odd_re], 0)


def times(a, b):
    a_re, a_im, b_re, b_im = a[:BLOCK], a[BLOCK:], b[:BLOCK], b[BLOCK:]
    return jnp.concatenate([a_re * b_re - a_im * b_im, a_re * b_im + a_im * b_re], 0)


def shifted_filter(frame, weights):
    return (
        weights[0:1] * frame
        + weights[1:2] * pltpu.roll(frame, 1, 0)
        + weights[2:3] * pltpu.roll(frame, 2, 0)
    )


def ahead_filter(frame, weights):
    rows = frame.shape[0]
    return (
        weights[0:1] * pltpu.roll(frame, rows - 2, 0)
        + weights[1:2] * pltpu.roll(frame, rows - 1, 0)
        + weights[2:3] * frame
    )


def rows_of(shape):
    return lax.broadcasted_iota(jnp.int32, shape, 0)


def over_channels(width, step):
    def one(i, _):
        step(pl.ds(pl.multiple_of(i * WIDTH, WIDTH), WIDTH), i * WIDTH)
        return 0

    lax.fori_loop(0, width // WIDTH, one, 0)


def sublane_sum(values):
    return jnp.sum(values, axis=0, keepdims=True)


def lane_parts(values):
    total = values[:, :LANES]
    for tile in range(1, values.shape[1] // LANES):
        total = total + values[:, tile * LANES : (tile + 1) * LANES]
    return total


def pack_kernel(
    key, value, gate, gate_long, key_long, short, out, tops, ends, taps, arrived
):
    rows, width = key.shape
    copies = []
    for chunk in range(width // WIDTH):
        here = pl.ds(chunk * WIDTH, WIDTH)
        pairs = [(short.at[1:3, :, here], taps.at[:, :, here])]
        for i, ref in enumerate((key, value)):
            pairs.append((ref.at[rows - EARLY :, here], tops.at[i, :, here]))
        for i, ref in enumerate((gate, gate_long, key_long)):
            pairs.append((ref.at[rows - RIM :, here], ends.at[i, :, here]))
        copies.append(
            [
                pltpu.make_async_copy(source, target, arrived.at[chunk, i])
                for i, (source, target) in enumerate(pairs)
            ]
        )
    for group in copies:
        for copy in group:
            copy.start()
    for chunk in range(width // WIDTH):
        here = pl.ds(chunk * WIDTH, WIDTH)
        for copy in copies[chunk]:
            copy.wait()
        key_part, value_part = tops[0, :, here].astype(F32), tops[1, :, here].astype(F32)
        product = ahead_filter(key_part, taps[0, :, here]) * ahead_filter(
            value_part, taps[1, :, here]
        )
        row = rows_of((TILE, WIDTH))
        key_end, value_end = key_part[-TILE:], value_part[-TILE:]
        gate_end, gate_long_end, key_long_end = (
            ends[i, :, here].astype(F32)[TILE:] for i in range(3)
        )
        first = jnp.where(
            row < 2,
            pltpu.roll(key_end, 2, 0),
            jnp.where(row < 4, pltpu.roll(value_end, 4, 0), gate_end),
        )
        second = jnp.where(
            row < 2,
            pltpu.roll(gate_long_end, 2, 0),
            jnp.where(row < 4, pltpu.roll(key_long_end, 4, 0), product[TILE:RIM]),
        )
        out[:, here] = jnp.concatenate([first, second, product[RIM:]], 0).astype(BF16)


def mode_tables(rates, mode, lanes, offset, sign):
    rate = jnp.broadcast_to(rates[mode : mode + 1, lanes], (TILE, LANES))
    row = rows_of((TILE, LANES)).astype(F32)
    return jnp.exp(-rate * (offset + sign * row)), jnp.exp(-TILE * rate)


def response(starts, steps, count, emit):
    parts = list(starts)
    for i in range(count):
        level = parts
        while len(level) > 1:
            level = [a + b for a, b in zip(level[::2], level[1::2])]
        emit(i, level[0])
        if i + 1 < count:
            parts = [part * step for part, step in zip(parts, steps)]


def lane_tiles(base):
    return [
        pl.ds(pl.multiple_of(base + tile * LANES, LANES), LANES) for tile in range(WIDTH // LANES)
    ]


def impulse_kernel(count, place, rates, weights, split_rows, long_hat, carry, leads, decays, impulse):
    modes, width = rates.shape
    rows = impulse.shape[0]
    for i, weight in enumerate(carry_weights(place[0], count, rows, rates[...])):
        carry[i] = weight

    def step(here, base):
        for tile, lanes in enumerate(lane_tiles(base)):
            starts, steps = [], []
            for mode in range(modes):
                lead, decay = mode_tables(rates, mode, lanes, 0.0, 1.0)
                start = lead * weights[mode : mode + 1, lanes]
                leads[mode, :, lanes] = start * jnp.exp(-rates[mode : mode + 1, lanes])
                decays[mode, :, lanes] = decay
                starts.append(start)
                steps.append(decay)

            def emit(i, total):
                impulse[i * TILE : (i + 1) * TILE, tile * LANES : (tile + 1) * LANES] = total

            response(starts, steps, rows // TILE, emit)
        for block in range(rows // BLOCK):
            long_hat[block, :, here] = forward_split(
                split_rows[...], impulse[block * BLOCK : (block + 1) * BLOCK]
            )
        for block in reversed(range(1, rows // BLOCK)):
            long_hat[block, :, here] = long_hat[block, :, here] + turned(
                long_hat[block - 1, :, here]
            )

    over_channels(width, step)


def own_kernel(
    gate, key, value, key_long, short, short_long, skip, taps, split_rows, exact_rows, backward, _,
    conv_early, gate_early, mixed_late, squares_late, key_feat, taps_hat, heads,
):
    rows, width = gate.shape
    squares_late[...] = jnp.zeros(squares_late.shape, F32)

    def step(here, base):
        hat = forward_split(split_rows[...], taps[:, here])
        taps_hat[:, here] = hat
        keys, values, gates, keys_long = (
            ref[:, here].astype(F32) for ref in (key, value, gate, key_long)
        )
        heads[:, here] = jnp.concatenate(
            [part[:TILE] for part in (keys, values, gates, keys_long)]
            + [taps[BLOCK - TILE :, here]],
            0,
        )
        product = shifted_filter(keys, short[1, :, here]) * shifted_filter(
            values, short[2, :, here]
        )
        row = rows_of((TILE, WIDTH))
        product = jnp.concatenate(
            [jnp.where(row < 2, 0.0, product[:TILE]), product[TILE:]], 0
        ).astype(BF16)
        before = None
        conv = []
        for block in range(rows // BLOCK):
            now = forward_exact(exact_rows[...], product[block * BLOCK : (block + 1) * BLOCK])
            window = now if before is None else now + turned(before)
            conv.append(backward_exact(backward[...], times(hat, window)))
            before = now
        total = jnp.concatenate(conv, 0) + skip[:, here] * product.astype(F32)
        feat = shifted_filter(gates, short[0, :, here])
        conv_early[:, here] = total[:EARLY]
        gate_early[:, here] = feat[:EARLY]
        mixed = (feat[EARLY:] * total[EARLY:]).astype(BF16)
        mixed_late[:, here] = mixed
        kept = mixed.astype(F32)
        squares_late[...] = squares_late[...] + lane_parts(kept * kept)
        key_feat[:, here] = shifted_filter(keys_long, short_long[1, :, here])

    over_channels(width, step)


def medium_kernel(
    halo, heads, short, skip, taps_hat, exact_rows, backward,
    conv_early, gate_early, mixed_late, squares_late,
    mixed, mixed_rim, squares, rim_long, total,
):
    width = halo.shape[1]
    total[...] = jnp.zeros(total.shape, F32)

    def step(here, base):
        halo_part = halo[:, here].astype(F32)
        rim, rim_late = halo_part[:TILE], halo_part[TILE:RIM]
        rim_long[:, here] = rim_late
        row = rows_of((TILE, WIDTH))
        key_part, value_part, gate_part, _, tail = (
            heads[i * TILE : (i + 1) * TILE, here] for i in range(5)
        )
        keys = jnp.where(row >= 6, pltpu.roll(key_part, 6, 0), pltpu.roll(rim, 4, 0))
        values = jnp.where(row >= 6, pltpu.roll(value_part, 6, 0), pltpu.roll(rim, 2, 0))
        start = shifted_filter(keys, short[1, :, here]) * shifted_filter(values, short[2, :, here])
        start = start.astype(BF16).astype(F32)
        end = jnp.where(row >= 6, start, halo_part[-TILE:])
        window = jnp.concatenate([halo_part[RIM:-TILE], end], 0).astype(BF16)
        spectrum = times(taps_hat[:, here], forward_exact(exact_rows[...], window))
        late = backward_exact(backward[...], spectrum)
        tap_a, tap_b, tap_c = (tail[i : i + 1] for i in (7, 6, 5))
        far_a, far_b, far_c = (rim_late[i : i + 1] for i in (5, 6, 7))
        skip_part = skip[:, here]
        rim_conv = late[TILE:RIM] + skip_part * pltpu.roll(end, 2, 0)
        rim_conv = rim_conv + jnp.where(
            row == 6, tap_a * far_a + tap_b * far_b + tap_c * far_c, tap_a * far_b + tap_b * far_c
        )
        rim_conv = jnp.where(row >= 6, rim_conv, 0.0)
        early = conv_early[:, here] + late[RIM:]
        extra = skip_part * jnp.where(row < 2, pltpu.roll(start, 2, 0), 0.0)
        extra = extra + jnp.where(row == 0, tap_a * far_c, 0.0)
        gates = shifted_filter(jnp.concatenate([rim, gate_part], 0), short[0, :, here])
        conv = jnp.concatenate([rim_conv, early[:TILE] + extra, early[TILE:]], 0)
        feat = jnp.concatenate([gates, gate_early[TILE:, here]], 0)
        kept = (feat * conv).astype(BF16).astype(F32)
        mixed[:EARLY, here] = kept[TILE:].astype(BF16)
        mixed[EARLY:, here] = mixed_late[:, here]
        mixed_rim[:, here] = kept[:TILE]
        total[...] = total[...] + lane_parts(kept * kept)

    over_channels(width, step)
    squares[...] = lax.dot_general(
        jnp.ones((TILE, LANES), F32),
        jnp.concatenate([total[...], squares_late[...]], 0),
        (((1,), (1,)), ((), ())),
        precision=lax.Precision.HIGHEST,
        preferred_element_type=F32,
    )


def value_kernel(mixed, mixed_rim, gain, key_feat, heads, rim_long, short, rates, parts, tails):
    rows, width = mixed.shape
    modes = rates.shape[0]

    def step(here, base):
        frame = jnp.concatenate([mixed_rim[:, here], mixed[:, here].astype(F32)], 0)
        keys = shifted_filter(
            jnp.concatenate(
                [pltpu.roll(rim_long[:, here], 4, 0), heads[3 * TILE : 4 * TILE, here]], 0
            ),
            short[1, :, here],
        )[TILE:]
        keys = jnp.concatenate([keys, key_feat[TILE:, here]], 0)
        weights = short[2, :, here] * gain[:, here]
        for j in range(3):
            moved = frame if j == 0 else pltpu.roll(frame, j, 0)
            parts[j, :, here] = keys * (weights[j : j + 1] * moved[TILE:])
        for lanes in lane_tiles(base):
            for mode in range(modes):
                tails[mode, :, lanes] = mode_tables(rates, mode, lanes, TILE - 1.0, -1.0)[0]

    over_channels(width, step)


def state_kernel(all_width, squares, parts, tails, decays, product_out, state, factors):
    rows, width = product_out.shape
    modes = decays.shape[0]
    factor = lax.rsqrt(squares[...] / all_width + 1e-06)
    high, rest = split(factor)
    low = (factor - high.astype(F32) - rest.astype(F32)).astype(BF16)
    row = rows_of(factor.shape)
    stack = jnp.where(row == 0, high.astype(F32), jnp.where(row == 1, rest.astype(F32), 0.0))
    stack = jnp.where(row == 2, low.astype(F32), stack)
    stack = jnp.concatenate([stack, jnp.zeros_like(stack)], 0).astype(BF16)
    inverse = lax.dot_general(
        stack,
        jnp.ones((RIM, LANES), BF16),
        (((0,), (0,)), ((), ())),
        preferred_element_type=F32,
    )
    factors[0] = inverse[TILE:]
    factors[1] = pltpu.roll(inverse, 1, 0)[TILE:]
    factors[2] = pltpu.roll(inverse, 2, 0)[TILE:]

    def step(here, base):
        for lanes in lane_tiles(base):
            steps = [decays[mode, :, lanes] for mode in range(modes)]
            held = None
            for i in range(0, rows, 2 * TILE):
                part = slice(i, i + 2 * TILE)
                product = (
                    parts[0, part, lanes] * factors[0, part]
                    + parts[1, part, lanes] * factors[1, part]
                    + parts[2, part, lanes] * factors[2, part]
                )
                product_out[part, lanes] = product.astype(BF16)
                for piece in (product[:TILE], product[TILE:]):
                    if held is None:
                        held = [piece] * modes
                    else:
                        held = [old * decay + piece for old, decay in zip(held, steps)]
            for mode in range(modes):
                state[mode : mode + 1, lanes] = sublane_sum(held[mode] * tails[mode, :, lanes])

    over_channels(width, step)


def local_kernel(product, long_hat, skip, exact_rows, backward, out, done):
    rows, width = product.shape
    done[...] = jnp.zeros(done.shape, F32)

    def step(here, base):
        spectra = []
        for block in range(rows // BLOCK):
            part = slice(block * BLOCK, (block + 1) * BLOCK)
            piece = product[part, here]
            spectra.append(forward_exact(exact_rows[...], piece))
            total = times(long_hat[0, :, here], spectra[block])
            for lag in range(1, block + 1):
                total = total + times(long_hat[lag, :, here], spectra[block - lag])
            out[part, here] = backward_exact(backward[...], total) + skip[:, here] * piece.astype(
                F32
            )

    over_channels(width, step)


def gate_kernel(gate_long, rim_long, short, mixed, _, gate_feat, mixed_out):
    width = gate_long.shape[1]

    def step(here, base):
        gates = jnp.concatenate(
            [pltpu.roll(rim_long[:, here], 6, 0), gate_long[:, here].astype(F32)], 0
        )
        gate_feat[:, here] = shifted_filter(gates, short[0, :, here])[TILE:]
        mixed_out[:, here] = mixed[:, here]

    over_channels(width, step)


def finish_kernel(state, decays, leads, local, gate_feat, out, held_out, sent):
    rows, width = local.shape
    modes = decays.shape[0]
    copies = []
    for chunk in range(width // PART):
        for tile in range(PART // LANES):
            lanes = slice(chunk * PART + tile * LANES, chunk * PART + (tile + 1) * LANES)
            starts = [
                leads[mode, :, lanes] * state[mode : mode + 1, lanes] for mode in range(modes)
            ]
            steps = [decays[mode, :, lanes] for mode in range(modes)]
            held = []

            def emit(i, total):
                part = slice(i * TILE, (i + 1) * TILE)
                held.append(gate_feat[part, lanes] * (local[part, lanes] + total))
                if i % 2 == 1:
                    held_out[(i - 1) * TILE : (i + 1) * TILE, lanes] = jnp.concatenate(
                        held[-2:], 0
                    ).astype(BF16)

            response(starts, steps, rows // TILE, emit)
        here = pl.ds(chunk * PART, PART)
        copy = pltpu.make_async_copy(held_out.at[:, here], out.at[:, here], sent.at[chunk])
        copy.start()
        copies.append(copy)
    for copy in copies:
        copy.wait()


SCALAR = pl.BlockSpec(memory_space=pltpu.SMEM)
KEPT = pl.BlockSpec(memory_space=pltpu.VMEM)
FAR = pl.BlockSpec(memory_space=pl.ANY)
MIB = 1024 * 1024


def call(kernel, name, in_specs, out_shape, scratch=(), flops=0, moved=0, room=12, out_specs=None):
    return pl.pallas_call(
        kernel,
        in_specs=in_specs,
        out_specs=out_specs or jax.tree.map(lambda _: KEPT, out_shape),
        out_shape=out_shape,
        scratch_shapes=list(scratch),
        compiler_params=pltpu.CompilerParams(vmem_limit_bytes=room * MIB),
        name=name,
        cost_estimate=pl.CostEstimate(flops=flops, bytes_accessed=moved, transcendentals=0),
    )


def in_hbm(value):
    return pltpu.with_memory_space_constraint(value, pltpu.HBM)


def arr(shape, dtype):
    return jax.ShapeDtypeStruct(shape, dtype)


def passed_along(value, axis, steps):
    count = lax.axis_size(axis)
    return lax.ppermute(value, axis, [(source, source + steps) for source in range(count - steps)])


def exchanged(value, axis, flip):
    count = lax.axis_size(axis)
    return lax.ppermute(value, axis, [(source, source ^ flip) for source in range(count)])


def stages(count):
    group = 1
    while group < count:
        radix = 4 if count // group >= 4 else 2
        yield group, radix
        group *= radix


def carry_weights(place, count, row_count, rates):
    for group, radix in stages(count):
        digit = (place // group) % radix
        within = (place % group).astype(F32)
        for turn in range(radix):
            member = digit ^ turn
            behind = (digit - 1 - member).astype(F32) * group + within
            decay = jnp.exp(-rates * (row_count * jnp.maximum(behind, 0.0)))
            yield jnp.where(member < digit, decay, 0.0)
            left = ((radix - 1 - member) * group).astype(F32)
            yield jnp.exp(-rates * (row_count * left))


def carried_state(state, weights, beside):
    count = lax.axis_size("ctx")
    incoming = jnp.zeros_like(state)
    sent = incoming
    at = 0
    for group, radix in stages(count):
        if group > 1 and group * radix == count:
            state = state + beside
        sent = state.astype(BF16)
        got = [state]
        for turn in range(1, radix):
            got.append(exchanged(sent, "ctx", turn * group).astype(F32))
        for turn in range(radix):
            incoming = incoming + weights[at + 2 * turn] * got[turn]
        state = sum(weights[at + 2 * turn + 1] * got[turn] for turn in range(radix))
        at += 2 * radix
    return incoming, sent


def body(
    gate_medium,
    key_medium,
    value_medium,
    short_medium,
    filter_medium,
    skip_medium,
    norm_gain,
    gate_long,
    key_long,
    short_long,
    decay_rates,
    residues,
    skip_long,
):
    rows, width = gate_medium.shape
    modes = decay_rates.shape[0]
    blocks = rows // BLOCK
    frame = rows + TILE
    count = lax.axis_size("ctx")
    all_width = width * lax.axis_size("ch")
    exact_rows, split_rows, backward, backward_late = (jnp.asarray(m) for m in transforms())
    far = [
        in_hbm(value)
        for value in (key_medium, value_medium, gate_medium, gate_long, key_long, short_medium)
    ]
    pack = call(
        pack_kernel, "pack", [FAR] * 6, arr((EARLY, width), BF16),
        [
            pltpu.VMEM((2, EARLY, width), BF16), pltpu.VMEM((3, RIM, width), BF16),
            pltpu.VMEM((2, 3, width), F32), pltpu.SemaphoreType.DMA((width // WIDTH, 6)),
        ],
    )(*far)
    halo = passed_along(pack, "ctx", 1)

    skip_row = skip_medium[None]
    mode_weight = residues * jnp.sqrt(-jnp.expm1(-2.0 * decay_rates))
    place = lax.axis_index("ctx").astype(jnp.int32).reshape(1)
    turns = sum(2 * radix for _, radix in stages(count)) or 1
    long_hat, carry, leads, decays = call(
        lambda *refs: impulse_kernel(count, *refs), "impulse",
        [SCALAR] + [KEPT] * 3,
        [
            arr((blocks, 2 * BLOCK, width), F32), arr((turns, modes, width), F32),
            arr((modes, TILE, width), F32), arr((modes, TILE, width), F32),
        ],
        [pltpu.VMEM((rows, WIDTH), F32)],
        flops=2000 * rows * width, moved=10 * rows * width,
    )(place, decay_rates, mode_weight, split_rows)

    conv_early, gate_early, mixed_late, squares_late, key_feat, taps_hat, heads = call(
        own_kernel, "own", [KEPT] * 12,
        [
            arr((EARLY, width), F32), arr((EARLY, width), F32),
            arr((rows - EARLY, width), BF16), arr((rows - EARLY, LANES), F32),
            arr((rows, width), F32), arr((2 * BLOCK, width), F32), arr((5 * TILE, width), F32),
        ],
        flops=2000 * rows * width, moved=10 * rows * width, room=16,
    )(
        gate_medium, key_medium, value_medium, key_long, short_medium, short_long, skip_row,
        filter_medium, split_rows, exact_rows, backward, carry,
    )

    mixed_medium, mixed_rim, squares, rim_long = call(
        medium_kernel, "medium", [KEPT] * 11,
        [
            arr((rows, width), BF16), arr((TILE, width), F32), arr((TILE, frame), F32),
            arr((TILE, width), F32),
        ],
        [pltpu.VMEM((EARLY + TILE, LANES), F32)],
        flops=1000 * rows * width, moved=10 * rows * width,
    )(
        halo, heads, short_medium, skip_row, taps_hat, exact_rows, backward_late,
        conv_early, gate_early, mixed_late, squares_late,
    )

    parts = [exchanged(squares, "ch", turn) for turn in range(1, lax.axis_size("ch"))]
    total_squares = squares
    for part in parts:
        total_squares = total_squares + part

    long_parts, tails = call(
        value_kernel, "value", [KEPT] * 8,
        [arr((3, rows, width), F32), arr((modes, TILE, width), F32)],
        flops=1000 * rows * width, moved=10 * rows * width,
    )(
        mixed_medium, mixed_rim, norm_gain[None], key_feat, heads, rim_long, short_long,
        decay_rates,
    )
    product_long, state = call(
        lambda *refs: state_kernel(all_width, *refs), "state", [KEPT] * 4,
        [arr((rows, width), BF16), arr((modes, width), F32)],
        [pltpu.VMEM((3, rows, LANES), F32)],
        flops=100 * rows * width, moved=10 * rows * width,
    )(total_squares, long_parts, tails, decays)

    local, done = call(
        local_kernel, "local", [KEPT] * 5, [arr((rows, width), F32), arr((1, width), F32)],
        flops=2000 * rows * width, moved=14 * rows * width,
    )(product_long, long_hat, skip_long[None], exact_rows, backward)
    incoming, last_sent = carried_state(state, carry, done)
    gate_feat, mixed_out = call(
        gate_kernel, "gate", [KEPT] * 5, [arr((rows, width), F32), arr((rows, width), BF16)],
        flops=1000 * rows * width, moved=14 * rows * width,
    )(gate_long, rim_long, short_long, mixed_medium, last_sent)
    mixed_long = call(
        finish_kernel, "finish", [KEPT] * 5, arr((rows, width), BF16),
        [pltpu.VMEM((rows, width), BF16), pltpu.SemaphoreType.DMA((width // PART,))], out_specs=FAR,
        flops=100 * rows * width, moved=8 * rows * width,
    )(incoming, decays, leads, local, gate_feat)
    return (mixed_out, mixed_long)


def solution(mesh):
    placed = (
        P("ctx", "ch"),
        P("ctx", "ch"),
        P("ctx", "ch"),
        P(None, None, "ch"),
        P(None, "ch"),
        P("ch"),
        P("ch"),
        P("ctx", "ch"),
        P("ctx", "ch"),
        P(None, None, "ch"),
        P(None, "ch"),
        P(None, "ch"),
        P("ch"),
    )
    return jax.shard_map(
        body,
        mesh=mesh,
        in_specs=placed,
        out_specs=(P("ctx", "ch"), P("ctx", "ch")),
        check_vma=False,
    )
```

```python
import jax
import jax.numpy as jnp
import ml_dtypes
import numpy as np
from jax import lax
from jax.experimental import pallas as pl
from jax.experimental.pallas import tpu as pltpu
from jax.sharding import PartitionSpec as P

F32 = jnp.float32
BF16 = jnp.bfloat16
BLOCK = 128
HALF = BLOCK // 2
TILE = 8
LANES = 128
WIDTH = 1024
PART = 512


RIM = 2 * TILE
EARLY = BLOCK + RIM


def split_np(values):
    high = values.astype(ml_dtypes.bfloat16)
    low = (values - high.astype(np.float64)).astype(ml_dtypes.bfloat16)
    return high, low


def angles(times):
    order = np.concatenate([np.arange(0, BLOCK, 2), np.arange(1, BLOCK, 2)])
    return np.pi * (order[:, None] + 0.5) * times[None, :] / BLOCK


def transforms():
    angle = angles(np.arange(BLOCK))
    forward = np.concatenate([np.cos(angle), -np.sin(angle)], 0)
    high, low = split_np(forward)
    exact_rows = np.concatenate([high, low], 1)
    split_rows = np.concatenate([high, high, low], 1)
    backward = np.concatenate(split_np(forward.T / BLOCK), 0)
    times = np.arange(-RIM, EARLY) + BLOCK - 2
    angle = angles(times)
    late = np.concatenate([np.cos(angle), -np.sin(angle)], 0).T / BLOCK
    late = late * ((times >= BLOCK - 4) & (times < 2 * BLOCK - 1))[:, None]
    return exact_rows, split_rows, backward, np.concatenate(split_np(late), 0)


def dot(a, b):
    return jnp.dot(a, b, preferred_element_type=F32)


def split(values):
    high = values.astype(BF16)
    return high, (values - high.astype(F32)).astype(BF16)


def forward_exact(matrix, block):
    return dot(matrix, jnp.concatenate([block, block], 0))


def forward_split(matrix, block):
    high, low = split(block)
    return dot(matrix, jnp.concatenate([high, low, high], 0))


def backward_exact(matrix, spectrum):
    rows = matrix.shape[0] // 2
    both = dot(matrix, spectrum.astype(BF16))
    return both[:rows] + both[rows:]


def turned(spectrum):
    even_re, odd_re, even_im, odd_im = (spectrum[i * HALF : (i + 1) * HALF] for i in range(4))
    return jnp.concatenate([-even_im, odd_im, even_re, -odd_re], 0)


def times(a, b):
    a_re, a_im, b_re, b_im = a[:BLOCK], a[BLOCK:], b[:BLOCK], b[BLOCK:]
    return jnp.concatenate([a_re * b_re - a_im * b_im, a_re * b_im + a_im * b_re], 0)


def shifted_filter(frame, weights):
    return (
        weights[0:1] * frame
        + weights[1:2] * pltpu.roll(frame, 1, 0)
        + weights[2:3] * pltpu.roll(frame, 2, 0)
    )


def ahead_filter(frame, weights):
    rows = frame.shape[0]
    return (
        weights[0:1] * pltpu.roll(frame, rows - 2, 0)
        + weights[1:2] * pltpu.roll(frame, rows - 1, 0)
        + weights[2:3] * frame
    )


def rows_of(shape):
    return lax.broadcasted_iota(jnp.int32, shape, 0)


def over_channels(width, step, unrolled=False):
    if unrolled:
        for i in range(width // WIDTH):
            step(pl.ds(i * WIDTH, WIDTH), i * WIDTH)
        return

    def one(i, _):
        step(pl.ds(pl.multiple_of(i * WIDTH, WIDTH), WIDTH), i * WIDTH)
        return 0

    lax.fori_loop(0, width // WIDTH, one, 0)


def sublane_sum(values):
    return jnp.sum(values, axis=0, keepdims=True)


def lane_parts(values):
    total = values[:, :LANES]
    for tile in range(1, values.shape[1] // LANES):
        total = total + values[:, tile * LANES : (tile + 1) * LANES]
    return total


def pack_kernel(
    key, value, gate, gate_long, key_long, short, out, tops, ends, taps, arrived
):
    rows, width = key.shape
    copies = []
    for chunk in range(width // WIDTH):
        here = pl.ds(chunk * WIDTH, WIDTH)
        pairs = [(short.at[1:3, :, here], taps.at[:, :, here])]
        for i, ref in enumerate((key, value)):
            pairs.append((ref.at[rows - EARLY :, here], tops.at[i, :, here]))
        for i, ref in enumerate((gate, gate_long, key_long)):
            pairs.append((ref.at[rows - RIM :, here], ends.at[i, :, here]))
        copies.append(
            [
                pltpu.make_async_copy(source, target, arrived.at[chunk, i])
                for i, (source, target) in enumerate(pairs)
            ]
        )
    for group in copies:
        for copy in group:
            copy.start()
    for chunk in range(width // WIDTH):
        here = pl.ds(chunk * WIDTH, WIDTH)
        for copy in copies[chunk]:
            copy.wait()
        key_part, value_part = tops[0, :, here].astype(F32), tops[1, :, here].astype(F32)
        product = ahead_filter(key_part, taps[0, :, here]) * ahead_filter(
            value_part, taps[1, :, here]
        )
        row = rows_of((TILE, WIDTH))
        key_end, value_end = key_part[-TILE:], value_part[-TILE:]
        gate_end, gate_long_end, key_long_end = (
            ends[i, :, here].astype(F32)[TILE:] for i in range(3)
        )
        first = jnp.where(
            row < 2,
            pltpu.roll(key_end, 2, 0),
            jnp.where(row < 4, pltpu.roll(value_end, 4, 0), gate_end),
        )
        second = jnp.where(
            row < 2,
            pltpu.roll(gate_long_end, 2, 0),
            jnp.where(row < 4, pltpu.roll(key_long_end, 4, 0), product[TILE:RIM]),
        )
        out[:, here] = jnp.concatenate([first, second, product[RIM:]], 0).astype(BF16)


def mode_tables(rates, mode, lanes, offset, sign):
    rate = jnp.broadcast_to(rates[mode : mode + 1, lanes], (TILE, LANES))
    row = rows_of((TILE, LANES)).astype(F32)
    return jnp.exp(-rate * (offset + sign * row)), jnp.exp(-TILE * rate)


def response(starts, steps, count, emit):
    parts = list(starts)
    for i in range(count):
        level = parts
        while len(level) > 1:
            level = [a + b for a, b in zip(level[::2], level[1::2])]
        emit(i, level[0])
        if i + 1 < count:
            parts = [part * step for part, step in zip(parts, steps)]


def lane_tiles(base):
    starts = [base + tile * LANES for tile in range(WIDTH // LANES)]
    if isinstance(base, int):
        return [pl.ds(start, LANES) for start in starts]
    return [pl.ds(pl.multiple_of(start, LANES), LANES) for start in starts]


def impulse_kernel(count, place, rates, weights, exact_rows, long_hat, carry, leads, decays, impulse):
    modes, width = rates.shape
    rows = impulse.shape[0]
    for i, weight in enumerate(carry_weights(place[0], count, rows, rates[...])):
        carry[i] = weight

    def step(here, base):
        for tile, lanes in enumerate(lane_tiles(base)):
            starts, steps = [], []
            for mode in range(modes):
                lead, decay = mode_tables(rates, mode, lanes, 0.0, 1.0)
                start = lead * weights[mode : mode + 1, lanes]
                leads[mode, :, lanes] = start * jnp.exp(-rates[mode : mode + 1, lanes])
                decays[mode, :, lanes] = decay
                starts.append(start)
                steps.append(decay)

            def emit(i, total):
                impulse[i * TILE : (i + 1) * TILE, tile * LANES : (tile + 1) * LANES] = total

            response(starts, steps, rows // TILE, emit)
        for block in range(rows // BLOCK):
            long_hat[block, :, here] = forward_exact(
                exact_rows[...], impulse[block * BLOCK : (block + 1) * BLOCK].astype(BF16)
            )
        for block in reversed(range(1, rows // BLOCK)):
            long_hat[block, :, here] = long_hat[block, :, here] + turned(
                long_hat[block - 1, :, here]
            )

    over_channels(width, step)


def own_kernel(
    gate, key, value, key_long, short, short_long, skip, taps, split_rows, exact_rows, backward, _,
    conv_early, gate_early, mixed_late, squares_late, key_feat, taps_hat, heads,
):
    rows, width = gate.shape
    squares_late[...] = jnp.zeros(squares_late.shape, F32)

    def step(here, base):
        hat = forward_split(split_rows[...], taps[:, here])
        taps_hat[:, here] = hat
        keys, values, gates, keys_long = (
            ref[:, here].astype(F32) for ref in (key, value, gate, key_long)
        )
        heads[:, here] = jnp.concatenate(
            [part[:TILE] for part in (keys, values, gates, keys_long)]
            + [taps[BLOCK - TILE :, here]],
            0,
        )
        product = shifted_filter(keys, short[1, :, here]) * shifted_filter(
            values, short[2, :, here]
        )
        row = rows_of((TILE, WIDTH))
        product = jnp.concatenate(
            [jnp.where(row < 2, 0.0, product[:TILE]), product[TILE:]], 0
        ).astype(BF16)
        before = None
        conv = []
        for block in range(rows // BLOCK):
            now = forward_exact(exact_rows[...], product[block * BLOCK : (block + 1) * BLOCK])
            window = now if before is None else now + turned(before)
            conv.append(backward_exact(backward[...], times(hat, window)))
            before = now
        total = jnp.concatenate(conv, 0) + skip[:, here] * product.astype(F32)
        feat = shifted_filter(gates, short[0, :, here])
        conv_early[:, here] = total[:EARLY]
        gate_early[:, here] = feat[:EARLY]
        mixed = (feat[EARLY:] * total[EARLY:]).astype(BF16)
        mixed_late[:, here] = mixed
        kept = mixed.astype(F32)
        squares_late[...] = squares_late[...] + lane_parts(kept * kept)
        key_feat[:, here] = shifted_filter(keys_long, short_long[1, :, here])

    over_channels(width, step)


def medium_kernel(
    halo, heads, short, skip, taps_hat, exact_rows, backward,
    conv_early, gate_early, mixed_late, squares_late,
    mixed, mixed_rim, squares, rim_long, total,
):
    width = halo.shape[1]
    total[...] = jnp.zeros(total.shape, F32)

    def step(here, base):
        halo_part = halo[:, here].astype(F32)
        rim, rim_late = halo_part[:TILE], halo_part[TILE:RIM]
        rim_long[:, here] = rim_late
        row = rows_of((TILE, WIDTH))
        key_part, value_part, gate_part, _, tail = (
            heads[i * TILE : (i + 1) * TILE, here] for i in range(5)
        )
        keys = jnp.where(row >= 6, pltpu.roll(key_part, 6, 0), pltpu.roll(rim, 4, 0))
        values = jnp.where(row >= 6, pltpu.roll(value_part, 6, 0), pltpu.roll(rim, 2, 0))
        start = shifted_filter(keys, short[1, :, here]) * shifted_filter(values, short[2, :, here])
        start = start.astype(BF16).astype(F32)
        end = jnp.where(row >= 6, start, halo_part[-TILE:])
        window = jnp.concatenate([halo_part[RIM:-TILE], end], 0).astype(BF16)
        spectrum = times(taps_hat[:, here], forward_exact(exact_rows[...], window))
        late = backward_exact(backward[...], spectrum)
        tap_a, tap_b, tap_c = (tail[i : i + 1] for i in (7, 6, 5))
        far_a, far_b, far_c = (rim_late[i : i + 1] for i in (5, 6, 7))
        skip_part = skip[:, here]
        rim_conv = late[TILE:RIM] + skip_part * pltpu.roll(end, 2, 0)
        rim_conv = rim_conv + jnp.where(
            row == 6, tap_a * far_a + tap_b * far_b + tap_c * far_c, tap_a * far_b + tap_b * far_c
        )
        rim_conv = jnp.where(row >= 6, rim_conv, 0.0)
        early = conv_early[:, here] + late[RIM:]
        extra = skip_part * jnp.where(row < 2, pltpu.roll(start, 2, 0), 0.0)
        extra = extra + jnp.where(row == 0, tap_a * far_c, 0.0)
        gates = shifted_filter(jnp.concatenate([rim, gate_part], 0), short[0, :, here])
        conv = jnp.concatenate([rim_conv, early[:TILE] + extra, early[TILE:]], 0)
        feat = jnp.concatenate([gates, gate_early[TILE:, here]], 0)
        kept = (feat * conv).astype(BF16).astype(F32)
        mixed[:EARLY, here] = kept[TILE:].astype(BF16)
        mixed[EARLY:, here] = mixed_late[:, here]
        mixed_rim[:, here] = kept[:TILE]
        total[...] = total[...] + lane_parts(kept * kept)

    over_channels(width, step, unrolled=True)
    squares[...] = lax.dot_general(
        jnp.ones((TILE, LANES), F32),
        jnp.concatenate([total[...], squares_late[...]], 0),
        (((1,), (1,)), ((), ())),
        precision=lax.Precision.HIGHEST,
        preferred_element_type=F32,
    )


def value_kernel(mixed, mixed_rim, gain, key_feat, heads, rim_long, short, rates, parts, tails):
    rows, width = mixed.shape
    modes = rates.shape[0]

    def step(here, base):
        frame = jnp.concatenate([mixed_rim[:, here], mixed[:, here].astype(F32)], 0)
        keys = shifted_filter(
            jnp.concatenate(
                [pltpu.roll(rim_long[:, here], 4, 0), heads[3 * TILE : 4 * TILE, here]], 0
            ),
            short[1, :, here],
        )[TILE:]
        keys = jnp.concatenate([keys, key_feat[TILE:, here]], 0)
        weights = short[2, :, here] * gain[:, here]
        for j in range(3):
            moved = frame if j == 0 else pltpu.roll(frame, j, 0)
            parts[j, :, here] = keys * (weights[j : j + 1] * moved[TILE:])
        for lanes in lane_tiles(base):
            for mode in range(modes):
                tails[mode, :, lanes] = mode_tables(rates, mode, lanes, TILE - 1.0, -1.0)[0]

    over_channels(width, step, unrolled=True)


def state_kernel(all_width, squares, parts, tails, decays, product_out, state, factors):
    rows, width = product_out.shape
    modes = decays.shape[0]
    factor = lax.rsqrt(squares[...] / all_width + 1e-06)
    high, rest = split(factor)
    low = (factor - high.astype(F32) - rest.astype(F32)).astype(BF16)
    row = rows_of(factor.shape)
    stack = jnp.where(row == 0, high.astype(F32), jnp.where(row == 1, rest.astype(F32), 0.0))
    stack = jnp.where(row == 2, low.astype(F32), stack)
    stack = jnp.concatenate([stack, jnp.zeros_like(stack)], 0).astype(BF16)
    inverse = lax.dot_general(
        stack,
        jnp.ones((RIM, LANES), BF16),
        (((0,), (0,)), ((), ())),
        preferred_element_type=F32,
    )
    factors[0] = inverse[TILE:]
    factors[1] = pltpu.roll(inverse, 1, 0)[TILE:]
    factors[2] = pltpu.roll(inverse, 2, 0)[TILE:]

    def step(here, base):
        for lanes in lane_tiles(base):
            steps = [decays[mode, :, lanes] for mode in range(modes)]
            held = None
            for i in range(0, rows, 2 * TILE):
                part = slice(i, i + 2 * TILE)
                product = (
                    parts[0, part, lanes] * factors[0, part]
                    + parts[1, part, lanes] * factors[1, part]
                    + parts[2, part, lanes] * factors[2, part]
                )
                product_out[part, lanes] = product.astype(BF16)
                for piece in (product[:TILE], product[TILE:]):
                    if held is None:
                        held = [piece] * modes
                    else:
                        held = [old * decay + piece for old, decay in zip(held, steps)]
            for mode in range(modes):
                state[mode : mode + 1, lanes] = sublane_sum(held[mode] * tails[mode, :, lanes])

    over_channels(width, step, unrolled=True)


def local_kernel(product, long_hat, skip, exact_rows, backward, out, done):
    rows, width = product.shape
    done[...] = jnp.zeros(done.shape, F32)

    def step(here, base):
        spectra = []
        for block in range(rows // BLOCK):
            part = slice(block * BLOCK, (block + 1) * BLOCK)
            piece = product[part, here]
            spectra.append(forward_exact(exact_rows[...], piece))
            total = times(long_hat[0, :, here], spectra[block])
            for lag in range(1, block + 1):
                total = total + times(long_hat[lag, :, here], spectra[block - lag])
            out[part, here] = backward_exact(backward[...], total) + skip[:, here] * piece.astype(
                F32
            )

    over_channels(width, step, unrolled=True)


def modal_tables(state, decays, leads, lanes):
    modes = decays.shape[0]
    starts = [leads[mode, :, lanes] * state[mode : mode + 1, lanes] for mode in range(modes)]
    return starts, [decays[mode, :, lanes] for mode in range(modes)]


def near_kernel(
    state, decays, leads, local, gate_long, rim_long, short, mixed, _,
    out, gate_feat, mixed_out, sent,
):
    rows, width = local.shape
    copy = pltpu.make_async_copy(mixed, mixed_out, sent)
    copy.start()

    def step(here, base):
        gates = jnp.concatenate(
            [pltpu.roll(rim_long[:, here], 6, 0), gate_long[:, here].astype(F32)], 0
        )
        gate_feat[:, here] = shifted_filter(gates, short[0, :, here])[TILE:]
        for lanes in lane_tiles(base):

            def emit(i, total):
                part = slice(i * TILE, (i + 1) * TILE)
                out[part, lanes] = gate_feat[part, lanes] * (local[part, lanes] + total)

            response(*modal_tables(state, decays, leads, lanes), rows // TILE, emit)

    over_channels(width, step, unrolled=True)
    copy.wait()


def finish_kernel(count, place, state, decays, leads, near, gate_feat, out, held_out, sent):
    rows, width = near.shape
    group, radix = list(stages(count))[-1] if count > 1 else (1, 1)
    later = (place[0] // group) % radix > 0
    copies = []
    for chunk in range(width // PART):
        here = pl.ds(chunk * PART, PART)

        @pl.when(later)
        def _():
            for tile in range(PART // LANES):
                lanes = slice(chunk * PART + tile * LANES, chunk * PART + (tile + 1) * LANES)
                held = []

                def emit(i, total):
                    part = slice(i * TILE, (i + 1) * TILE)
                    held.append(near[part, lanes] + gate_feat[part, lanes] * total)
                    if i % 2 == 1:
                        held_out[(i - 1) * TILE : (i + 1) * TILE, lanes] = jnp.concatenate(
                            held[-2:], 0
                        ).astype(BF16)

                response(*modal_tables(state, decays, leads, lanes), rows // TILE, emit)

        @pl.when(jnp.logical_not(later))
        def _():
            held_out[:, here] = near[:, here].astype(BF16)

        copy = pltpu.make_async_copy(held_out.at[:, here], out.at[:, here], sent.at[chunk])
        copy.start()
        copies.append(copy)
    for copy in copies:
        copy.wait()


SCALAR = pl.BlockSpec(memory_space=pltpu.SMEM)
KEPT = pl.BlockSpec(memory_space=pltpu.VMEM)
FAR = pl.BlockSpec(memory_space=pl.ANY)
MIB = 1024 * 1024


def call(kernel, name, in_specs, out_shape, scratch=(), flops=0, moved=0, room=12, out_specs=None):
    return pl.pallas_call(
        kernel,
        in_specs=in_specs,
        out_specs=out_specs or jax.tree.map(lambda _: KEPT, out_shape),
        out_shape=out_shape,
        scratch_shapes=list(scratch),
        compiler_params=pltpu.CompilerParams(vmem_limit_bytes=room * MIB),
        name=name,
        cost_estimate=pl.CostEstimate(flops=flops, bytes_accessed=moved, transcendentals=0),
    )


def in_hbm(value):
    return pltpu.with_memory_space_constraint(value, pltpu.HBM)


def arr(shape, dtype):
    return jax.ShapeDtypeStruct(shape, dtype)


def passed_along(value, axis, steps):
    count = lax.axis_size(axis)
    return lax.ppermute(value, axis, [(source, source + steps) for source in range(count - steps)])


def exchanged(value, axis, flip):
    count = lax.axis_size(axis)
    return lax.ppermute(value, axis, [(source, source ^ flip) for source in range(count)])


def stages(count):
    group = 1
    while group < count:
        radix = 4 if count // group >= 4 else 2
        yield group, radix
        group *= radix


def carry_weights(place, count, row_count, rates):
    for group, radix in stages(count):
        digit = (place // group) % radix
        within = (place % group).astype(F32)
        for turn in range(radix):
            member = digit ^ turn
            behind = (digit - 1 - member).astype(F32) * group + within
            decay = jnp.exp(-rates * (row_count * jnp.maximum(behind, 0.0)))
            yield jnp.where(member < digit, decay, 0.0)
            left = ((radix - 1 - member) * group).astype(F32)
            yield jnp.exp(-rates * (row_count * left))


def carried_state(state, weights, beside):
    count = lax.axis_size("ctx")
    known = incoming = jnp.zeros_like(state)
    sent = state
    at = 0
    for group, radix in stages(count):
        known = known + incoming
        if group > 1 and group * radix == count:
            state = state + beside
        sent = state.astype(BF16)
        got = [state]
        for turn in range(1, radix):
            got.append(exchanged(sent, "ctx", turn * group).astype(F32))
        incoming = sum(weights[at + 2 * turn] * got[turn] for turn in range(radix))
        state = sum(weights[at + 2 * turn + 1] * got[turn] for turn in range(radix))
        at += 2 * radix
    return known, incoming, sent


def body(
    gate_medium,
    key_medium,
    value_medium,
    short_medium,
    filter_medium,
    skip_medium,
    norm_gain,
    gate_long,
    key_long,
    short_long,
    decay_rates,
    residues,
    skip_long,
):
    rows, width = gate_medium.shape
    modes = decay_rates.shape[0]
    blocks = rows // BLOCK
    frame = rows + TILE
    count = lax.axis_size("ctx")
    all_width = width * lax.axis_size("ch")
    exact_rows, split_rows, backward, backward_late = (jnp.asarray(m) for m in transforms())
    far = [
        in_hbm(value)
        for value in (key_medium, value_medium, gate_medium, gate_long, key_long, short_medium)
    ]
    place = lax.axis_index("ctx").astype(jnp.int32).reshape(1)
    pack = call(
        pack_kernel, "pack", [FAR] * 6, arr((EARLY, width), BF16),
        [
            pltpu.VMEM((2, EARLY, width), BF16), pltpu.VMEM((3, RIM, width), BF16),
            pltpu.VMEM((2, 3, width), F32), pltpu.SemaphoreType.DMA((width // WIDTH, 6)),
        ],
    )(*far)
    halo = passed_along(pack, "ctx", 1)

    skip_row = skip_medium[None]
    mode_weight = residues * jnp.sqrt(-jnp.expm1(-2.0 * decay_rates))
    turns = sum(2 * radix for _, radix in stages(count)) or 1
    long_hat, carry, leads, decays = call(
        lambda *refs: impulse_kernel(count, *refs), "impulse",
        [SCALAR] + [KEPT] * 3,
        [
            arr((blocks, 2 * BLOCK, width), F32), arr((turns, modes, width), F32),
            arr((modes, TILE, width), F32), arr((modes, TILE, width), F32),
        ],
        [pltpu.VMEM((rows, WIDTH), F32)],
        flops=2000 * rows * width, moved=10 * rows * width,
    )(place, decay_rates, mode_weight, exact_rows)

    conv_early, gate_early, mixed_late, squares_late, key_feat, taps_hat, heads = call(
        own_kernel, "own", [KEPT] * 12,
        [
            arr((EARLY, width), F32), arr((EARLY, width), F32),
            arr((rows - EARLY, width), BF16), arr((rows - EARLY, LANES), F32),
            arr((rows, width), F32), arr((2 * BLOCK, width), F32), arr((5 * TILE, width), F32),
        ],
        flops=2000 * rows * width, moved=10 * rows * width, room=16,
    )(
        gate_medium, key_medium, value_medium, key_long, short_medium, short_long, skip_row,
        filter_medium, split_rows, exact_rows, backward, carry,
    )

    mixed_medium, mixed_rim, squares, rim_long = call(
        medium_kernel, "medium", [KEPT] * 11,
        [
            arr((rows, width), BF16), arr((TILE, width), F32), arr((TILE, frame), F32),
            arr((TILE, width), F32),
        ],
        [pltpu.VMEM((EARLY + TILE, LANES), F32)],
        flops=1000 * rows * width, moved=10 * rows * width,
    )(
        halo, heads, short_medium, skip_row, taps_hat, exact_rows, backward_late,
        conv_early, gate_early, mixed_late, squares_late,
    )

    parts = [exchanged(squares, "ch", turn) for turn in range(1, lax.axis_size("ch"))]
    total_squares = squares
    for part in parts:
        total_squares = total_squares + part

    long_parts, tails = call(
        value_kernel, "value", [KEPT] * 8,
        [arr((3, rows, width), F32), arr((modes, TILE, width), F32)],
        flops=1000 * rows * width, moved=10 * rows * width,
    )(
        mixed_medium, mixed_rim, norm_gain[None], key_feat, heads, rim_long, short_long,
        decay_rates,
    )
    product_long, state = call(
        lambda *refs: state_kernel(all_width, *refs), "state", [KEPT] * 4,
        [arr((rows, width), BF16), arr((modes, width), F32)],
        [pltpu.VMEM((3, rows, LANES), F32)],
        flops=100 * rows * width, moved=10 * rows * width,
    )(total_squares, long_parts, tails, decays)

    local, done = call(
        local_kernel, "local", [KEPT] * 5, [arr((rows, width), F32), arr((1, width), F32)],
        flops=2000 * rows * width, moved=14 * rows * width,
    )(product_long, long_hat, skip_long[None], exact_rows, backward)
    known, incoming, last_sent = carried_state(state, carry, done)
    near, gate_feat, mixed_out = call(
        near_kernel, "near", [KEPT] * 9,
        [arr((rows, width), F32), arr((rows, width), F32), arr((rows, width), BF16)],
        [pltpu.SemaphoreType.DMA], out_specs=[KEPT, KEPT, FAR],
        flops=1000 * rows * width, moved=14 * rows * width,
    )(known, decays, leads, local, gate_long, rim_long, short_long, mixed_medium, last_sent)
    mixed_long = call(
        lambda *refs: finish_kernel(count, *refs), "finish", [SCALAR] + [KEPT] * 5,
        arr((rows, width), BF16),
        [pltpu.VMEM((rows, width), BF16), pltpu.SemaphoreType.DMA((width // PART,))], out_specs=FAR,
        flops=100 * rows * width, moved=8 * rows * width,
    )(place, incoming, decays, leads, near, gate_feat)
    return (mixed_out, mixed_long)


def solution(mesh):
    placed = (
        P("ctx", "ch"),
        P("ctx", "ch"),
        P("ctx", "ch"),
        P(None, None, "ch"),
        P(None, "ch"),
        P("ch"),
        P("ch"),
        P("ctx", "ch"),
        P("ctx", "ch"),
        P(None, None, "ch"),
        P(None, "ch"),
        P(None, "ch"),
        P("ch"),
    )
    return jax.shard_map(
        body,
        mesh=mesh,
        in_specs=placed,
        out_specs=(P("ctx", "ch"), P("ctx", "ch")),
        check_vma=False,
    )
```

```python
import jax
import jax.numpy as jnp
import ml_dtypes
import numpy as np
from jax import lax
from jax.experimental import pallas as pl
from jax.experimental.pallas import tpu as pltpu
from jax.sharding import PartitionSpec as P

F32 = jnp.float32
BF16 = jnp.bfloat16
BLOCK = 128
HALF = BLOCK // 2
TILE = 8
LANES = 128
WIDTH = 1024
PART = 512


RIM = 2 * TILE
EARLY = BLOCK + RIM
TURN = EARLY + RIM


def split_np(values):
    high = values.astype(ml_dtypes.bfloat16)
    low = (values - high.astype(np.float64)).astype(ml_dtypes.bfloat16)
    return high, low


def angles(times):
    order = np.concatenate([np.arange(0, BLOCK, 2), np.arange(1, BLOCK, 2)])
    return np.pi * (order[:, None] + 0.5) * times[None, :] / BLOCK


def transforms():
    angle = angles(np.arange(BLOCK))
    forward = np.concatenate([np.cos(angle), -np.sin(angle)], 0)
    high, low = split_np(forward)
    exact_rows = np.concatenate([high, low], 1)
    split_rows = np.concatenate([high, high, low], 1)
    backward = np.concatenate(split_np(forward.T / BLOCK), 0)
    times = np.arange(-RIM, EARLY) + BLOCK - 2
    angle = angles(times)
    late = np.concatenate([np.cos(angle), -np.sin(angle)], 0).T / BLOCK
    late = late * ((times >= BLOCK - 4) & (times < 2 * BLOCK - 1))[:, None]
    return exact_rows, split_rows, backward, np.concatenate(split_np(late), 0)


def dot(a, b):
    return jnp.dot(a, b, preferred_element_type=F32)


def split(values):
    high = values.astype(BF16)
    return high, (values - high.astype(F32)).astype(BF16)


def forward_exact(matrix, block):
    return dot(matrix, jnp.concatenate([block, block], 0))


def forward_split(matrix, block):
    high, low = split(block)
    return dot(matrix, jnp.concatenate([high, low, high], 0))


def backward_exact(matrix, spectrum):
    rows = matrix.shape[0] // 2
    both = dot(matrix, spectrum.astype(BF16))
    return both[:rows] + both[rows:]


def turned(spectrum):
    even_re, odd_re, even_im, odd_im = (spectrum[i * HALF : (i + 1) * HALF] for i in range(4))
    return jnp.concatenate([-even_im, odd_im, even_re, -odd_re], 0)


def times(a, b):
    a_re, a_im, b_re, b_im = a[:BLOCK], a[BLOCK:], b[:BLOCK], b[BLOCK:]
    return jnp.concatenate([a_re * b_re - a_im * b_im, a_re * b_im + a_im * b_re], 0)


def shifted_filter(frame, weights):
    return (
        weights[0:1] * frame
        + weights[1:2] * pltpu.roll(frame, 1, 0)
        + weights[2:3] * pltpu.roll(frame, 2, 0)
    )


def ahead_filter(frame, weights):
    rows = frame.shape[0]
    return (
        weights[0:1] * pltpu.roll(frame, rows - 2, 0)
        + weights[1:2] * pltpu.roll(frame, rows - 1, 0)
        + weights[2:3] * frame
    )


def rows_of(shape):
    return lax.broadcasted_iota(jnp.int32, shape, 0)


def over_channels(width, step, unrolled=False):
    if unrolled:
        for i in range(width // WIDTH):
            step(pl.ds(i * WIDTH, WIDTH), i * WIDTH)
        return

    def one(i, _):
        step(pl.ds(pl.multiple_of(i * WIDTH, WIDTH), WIDTH), i * WIDTH)
        return 0

    lax.fori_loop(0, width // WIDTH, one, 0)


def sublane_sum(values):
    return jnp.sum(values, axis=0, keepdims=True)


def lane_parts(values):
    total = values[:, :LANES]
    for tile in range(1, values.shape[1] // LANES):
        total = total + values[:, tile * LANES : (tile + 1) * LANES]
    return total


def row_sums(partial):
    return lax.dot_general(
        jnp.ones((TILE, LANES), F32),
        partial,
        (((1,), (1,)), ((), ())),
        precision=lax.Precision.HIGHEST,
        preferred_element_type=F32,
    )


def norm_factors(squares, all_width):
    factor = lax.rsqrt(squares / all_width + 1e-06)
    high, rest = split(factor)
    low = (factor - high.astype(F32) - rest.astype(F32)).astype(BF16)
    row = rows_of(factor.shape)
    stack = jnp.where(row == 0, high.astype(F32), jnp.where(row == 1, rest.astype(F32), 0.0))
    stack = jnp.where(row == 2, low.astype(F32), stack)
    stack = jnp.concatenate([stack, jnp.zeros_like(stack)], 0).astype(BF16)
    return lax.dot_general(
        stack,
        jnp.ones((RIM, LANES), BF16),
        (((0,), (0,)), ((), ())),
        preferred_element_type=F32,
    )


def pack_kernel(
    _, key, value, gate, gate_long, key_long, short, out, tops, ends, taps, arrived
):
    rows, width = key.shape
    copies = []
    for chunk in range(width // WIDTH):
        here = pl.ds(chunk * WIDTH, WIDTH)
        pairs = [(short.at[1:3, :, here], taps.at[:, :, here])]
        for i, ref in enumerate((key, value)):
            pairs.append((ref.at[rows - EARLY :, here], tops.at[i, :, here]))
        for i, ref in enumerate((gate, gate_long, key_long)):
            pairs.append((ref.at[rows - RIM :, here], ends.at[i, :, here]))
        copies.append(
            [
                pltpu.make_async_copy(source, target, arrived.at[chunk, i])
                for i, (source, target) in enumerate(pairs)
            ]
        )
    for group in copies:
        for copy in group:
            copy.start()
    for chunk in range(width // WIDTH):
        here = pl.ds(chunk * WIDTH, WIDTH)
        for copy in copies[chunk]:
            copy.wait()
        for lanes in lane_tiles(chunk * WIDTH):
            key_part, value_part = tops[0, :, lanes].astype(F32), tops[1, :, lanes].astype(F32)
            product = ahead_filter(key_part, taps[0, :, lanes]) * ahead_filter(
                value_part, taps[1, :, lanes]
            )
            row = rows_of((TILE, LANES))
            gate_end, gate_long_end, key_long_end = (
                ends[i, :, lanes].astype(F32)[TILE:] for i in range(3)
            )
            first = jnp.where(
                row < 2,
                pltpu.roll(key_part[-TILE:], 2, 0),
                jnp.where(row < 4, pltpu.roll(value_part[-TILE:], 4, 0), gate_end),
            )
            second = jnp.where(
                row < 2,
                pltpu.roll(gate_long_end, 2, 0),
                jnp.where(row < 4, pltpu.roll(key_long_end, 4, 0), product[TILE:RIM]),
            )
            out[:, lanes] = jnp.concatenate([first, second, product[RIM:]], 0).astype(BF16)


def mode_tables(rates, mode, lanes, offset, sign):
    rate = jnp.broadcast_to(rates[mode : mode + 1, lanes], (TILE, LANES))
    row = rows_of((TILE, LANES)).astype(F32)
    return jnp.exp(-rate * (offset + sign * row)), jnp.exp(-TILE * rate)


def response(starts, steps, count, emit):
    parts = list(starts)
    for i in range(count):
        level = parts
        while len(level) > 1:
            level = [a + b for a, b in zip(level[::2], level[1::2])]
        emit(i, level[0])
        if i + 1 < count:
            parts = [part * step for part, step in zip(parts, steps)]


def lane_tiles(base):
    starts = [base + tile * LANES for tile in range(WIDTH // LANES)]
    if isinstance(base, int):
        return [pl.ds(start, LANES) for start in starts]
    return [pl.ds(pl.multiple_of(start, LANES), LANES) for start in starts]


def impulse_kernel(
    count, place, rates, weights, exact_rows, _, long_hat, carry, leads, decays, tails, impulse
):
    modes, width = rates.shape
    rows = impulse.shape[0]
    for i, weight in enumerate(carry_weights(place[0], count, rows, rates[...])):
        carry[i] = weight

    def step(here, base):
        for tile, lanes in enumerate(lane_tiles(base)):
            starts, steps = [], []
            for mode in range(modes):
                lead, decay = mode_tables(rates, mode, lanes, 0.0, 1.0)
                start = lead * weights[mode : mode + 1, lanes]
                leads[mode, :, lanes] = start * jnp.exp(-rates[mode : mode + 1, lanes])
                decays[mode, :, lanes] = decay
                tails[mode, :, lanes] = mode_tables(rates, mode, lanes, TILE - 1.0, -1.0)[0]
                starts.append(start)
                steps.append(decay)

            def emit(i, total):
                impulse[i * TILE : (i + 1) * TILE, tile * LANES : (tile + 1) * LANES] = total

            response(starts, steps, rows // TILE, emit)
        for block in range(rows // BLOCK):
            long_hat[block, :, here] = forward_exact(
                exact_rows[...], impulse[block * BLOCK : (block + 1) * BLOCK].astype(BF16)
            )
        for block in reversed(range(1, rows // BLOCK)):
            long_hat[block, :, here] = long_hat[block, :, here] + turned(
                long_hat[block - 1, :, here]
            )

    over_channels(width, step)


def own_kernel(
    gate, key, value, short, skip, taps, split_rows, exact_rows, backward, _,
    conv_early, gate_early, mixed_late, squares_late, taps_hat, heads, sums,
):
    rows, width = gate.shape
    sums[...] = jnp.zeros(sums.shape, F32)

    def step(here, base):
        hat = forward_split(split_rows[...], taps[:, here])
        taps_hat[:, here] = hat
        keys, values, gates = (ref[:, here].astype(F32) for ref in (key, value, gate))
        heads[:, here] = jnp.concatenate(
            [part[:TILE] for part in (keys, values, gates)]
            + [taps[BLOCK - TILE :, here]],
            0,
        )
        product = shifted_filter(keys, short[1, :, here]) * shifted_filter(
            values, short[2, :, here]
        )
        row = rows_of((TILE, WIDTH))
        product = jnp.concatenate(
            [jnp.where(row < 2, 0.0, product[:TILE]), product[TILE:]], 0
        ).astype(BF16)
        before = None
        conv = []
        for block in range(rows // BLOCK):
            now = forward_exact(exact_rows[...], product[block * BLOCK : (block + 1) * BLOCK])
            window = now if before is None else now + turned(before)
            conv.append(backward_exact(backward[...], times(hat, window)))
            before = now
        total = jnp.concatenate(conv, 0) + skip[:, here] * product.astype(F32)
        feat = shifted_filter(gates, short[0, :, here])
        conv_early[:, here] = total[:EARLY]
        gate_early[:, here] = feat[:EARLY]
        mixed = (feat[EARLY:] * total[EARLY:]).astype(BF16)
        mixed_late[:, here] = mixed
        kept = mixed.astype(F32)
        sums[...] = sums[...] + lane_parts(kept * kept)

    over_channels(width, step)
    squares_late[...] = row_sums(sums[...])


def medium_kernel(
    halo, heads, short, skip, taps_hat, exact_rows, backward,
    conv_early, gate_early, mixed_late, _, __,
    mixed, mixed_rim, squares, rim_long, total,
):
    width = halo.shape[1]
    total[...] = jnp.zeros(total.shape, F32)

    def step(here, base):
        halo_part = halo[:, here].astype(F32)
        rim, rim_late = halo_part[:TILE], halo_part[TILE:RIM]
        rim_long[:, here] = rim_late
        row = rows_of((TILE, WIDTH))
        key_part, value_part, gate_part, tail = (
            heads[i * TILE : (i + 1) * TILE, here] for i in range(4)
        )
        keys = jnp.where(row >= 6, pltpu.roll(key_part, 6, 0), pltpu.roll(rim, 4, 0))
        values = jnp.where(row >= 6, pltpu.roll(value_part, 6, 0), pltpu.roll(rim, 2, 0))
        start = shifted_filter(keys, short[1, :, here]) * shifted_filter(values, short[2, :, here])
        start = start.astype(BF16).astype(F32)
        end = jnp.where(row >= 6, start, halo_part[-TILE:])
        window = jnp.concatenate([halo_part[RIM:-TILE], end], 0).astype(BF16)
        spectrum = times(taps_hat[:, here], forward_exact(exact_rows[...], window))
        late = backward_exact(backward[...], spectrum)
        tap_a, tap_b, tap_c = (tail[i : i + 1] for i in (7, 6, 5))
        far_a, far_b, far_c = (rim_late[i : i + 1] for i in (5, 6, 7))
        skip_part = skip[:, here]
        rim_conv = late[TILE:RIM] + skip_part * pltpu.roll(end, 2, 0)
        rim_conv = rim_conv + jnp.where(
            row == 6, tap_a * far_a + tap_b * far_b + tap_c * far_c, tap_a * far_b + tap_b * far_c
        )
        rim_conv = jnp.where(row >= 6, rim_conv, 0.0)
        early = conv_early[:, here] + late[RIM:]
        extra = skip_part * jnp.where(row < 2, pltpu.roll(start, 2, 0), 0.0)
        extra = extra + jnp.where(row == 0, tap_a * far_c, 0.0)
        gates = shifted_filter(jnp.concatenate([rim, gate_part], 0), short[0, :, here])
        conv = jnp.concatenate([rim_conv, early[:TILE] + extra, early[TILE:]], 0)
        feat = jnp.concatenate([gates, gate_early[TILE:, here]], 0)
        kept = (feat * conv).astype(BF16).astype(F32)
        mixed[:EARLY, here] = kept[TILE:].astype(BF16)
        mixed[EARLY:, here] = mixed_late[:, here]
        mixed_rim[:, here] = kept[:TILE]
        total[...] = total[...] + lane_parts(kept * kept)

    over_channels(width, step, unrolled=True)
    squares[...] = row_sums(total[...])


def late_kernel(
    all_width, squares, mixed_late, key_long, gain, short, decays, tails, product_out, state
):
    rows, width = key_long.shape
    modes = decays.shape[0]
    factors = norm_factors(squares[...], all_width)

    def step(here, base):
        for lanes in lane_tiles(base):
            frame = mixed_late[:, lanes].astype(F32) * factors
            feat = shifted_filter(frame, short[2, :, lanes] * gain[:, lanes])
            keys = shifted_filter(key_long[EARLY:, lanes].astype(F32), short[1, :, lanes])
            product = (keys * feat)[TURN - EARLY :]
            product_out[:, lanes] = product.astype(BF16)
            held = [product[:TILE]] * modes
            steps = [decays[mode, :, lanes] for mode in range(modes)]
            for i in range(TILE, rows - TURN, TILE):
                held = [old * decay + product[i : i + TILE] for old, decay in zip(held, steps)]
            for mode in range(modes):
                state[mode : mode + 1, lanes] = sublane_sum(held[mode] * tails[mode, :, lanes])

    over_channels(width, step, unrolled=True)


def value_kernel(
    mixed, mixed_rim, gain, key_long, rim_long, short, rates, tails, parts, tails_far
):
    rows, width = mixed.shape
    modes = rates.shape[0]

    def step(here, base):
        frame = jnp.concatenate([mixed_rim[:, here], mixed[:TURN, here].astype(F32)], 0)
        keys = shifted_filter(
            jnp.concatenate(
                [pltpu.roll(rim_long[:, here], 4, 0), key_long[:TURN, here].astype(F32)], 0
            ),
            short[1, :, here],
        )[TILE:]
        weights = short[2, :, here] * gain[:, here]
        for j in range(3):
            moved = frame if j == 0 else pltpu.roll(frame, j, 0)
            parts[j, :, here] = keys * (weights[j : j + 1] * moved[TILE:])
        for mode in range(modes):
            tails_far[mode, :, here] = tails[mode, :, here] * jnp.exp(
                (TURN - rows) * rates[mode : mode + 1, here]
            )

    over_channels(width, step, unrolled=True)


def state_kernel(
    all_width, squares, squares_late, parts, tails_far, decays, state_late,
    product_out, state, factors,
):
    width = product_out.shape[1]
    modes = decays.shape[0]
    inverse = norm_factors(squares[...], all_width)
    inverse = jnp.concatenate(
        [inverse, norm_factors(squares_late[...], all_width)[: TURN - EARLY]], 0
    )
    factors[0] = inverse[TILE:]
    factors[1] = pltpu.roll(inverse, 1, 0)[TILE:]
    factors[2] = pltpu.roll(inverse, 2, 0)[TILE:]

    def step(here, base):
        for lanes in lane_tiles(base):
            steps = [decays[mode, :, lanes] for mode in range(modes)]
            held = None
            for i in range(0, TURN, 2 * TILE):
                part = slice(i, i + 2 * TILE)
                product = (
                    parts[0, part, lanes] * factors[0, part]
                    + parts[1, part, lanes] * factors[1, part]
                    + parts[2, part, lanes] * factors[2, part]
                )
                product_out[part, lanes] = product.astype(BF16)
                for piece in (product[:TILE], product[TILE:]):
                    if held is None:
                        held = [piece] * modes
                    else:
                        held = [old * decay + piece for old, decay in zip(held, steps)]
            for mode in range(modes):
                state[mode : mode + 1, lanes] = state_late[mode : mode + 1, lanes] + sublane_sum(
                    held[mode] * tails_far[mode, :, lanes]
                )

    over_channels(width, step, unrolled=True)


def local_kernel(early, late, long_hat, skip, exact_rows, backward, out, done):
    rows, width = out.shape
    done[...] = jnp.zeros(done.shape, F32)

    def step(here, base):
        spectra = []
        product = jnp.concatenate([early[:, here].astype(F32), late[:, here].astype(F32)], 0)
        for block in range(rows // BLOCK):
            part = slice(block * BLOCK, (block + 1) * BLOCK)
            piece = product[part]
            spectra.append(forward_exact(exact_rows[...], piece.astype(BF16)))
            total = times(long_hat[0, :, here], spectra[block])
            for lag in range(1, block + 1):
                total = total + times(long_hat[lag, :, here], spectra[block - lag])
            out[part, here] = backward_exact(backward[...], total) + skip[:, here] * piece

    over_channels(width, step, unrolled=True)


def modal_tables(state, decays, leads, lanes):
    modes = decays.shape[0]
    starts = [leads[mode, :, lanes] * state[mode : mode + 1, lanes] for mode in range(modes)]
    return starts, [decays[mode, :, lanes] for mode in range(modes)]


def near_kernel(
    state, decays, leads, local, gate_long, rim_long, short, mixed, _,
    near, gate_feat, mixed_out, out, held_out, sent,
):
    rows, width = local.shape
    copies = [pltpu.make_async_copy(mixed, mixed_out, sent.at[width // WIDTH])]
    copies[0].start()

    def step(here, base):
        gates = jnp.concatenate(
            [pltpu.roll(rim_long[:, here], 6, 0), gate_long[:, here].astype(F32)], 0
        )
        gate_feat[:, here] = shifted_filter(gates, short[0, :, here])[TILE:]
        for lanes in lane_tiles(base):

            held = []

            def emit(i, total):
                part = slice(i * TILE, (i + 1) * TILE)
                held.append(gate_feat[part, lanes] * (local[part, lanes] + total))
                near[part, lanes] = held[-1]
                if i % 2 == 1:
                    held_out[(i - 1) * TILE : (i + 1) * TILE, lanes] = jnp.concatenate(
                        held[-2:], 0
                    ).astype(BF16)

            response(*modal_tables(state, decays, leads, lanes), rows // TILE, emit)
        copy = pltpu.make_async_copy(
            held_out.at[:, here], out.at[:, here], sent.at[base // WIDTH]
        )
        copy.start()
        copies.append(copy)

    over_channels(width, step, unrolled=True)
    for copy in copies:
        copy.wait()


def finish_kernel(count, place, state, decays, leads, near, gate_feat, _, out, held_out, sent):
    rows, width = near.shape
    group, radix = list(stages(count))[-1] if count > 1 else (1, 1)

    @pl.when((place[0] // group) % radix > 0)
    def _():
        copies = []
        for chunk in range(width // PART):
            here = pl.ds(chunk * PART, PART)
            for tile in range(PART // LANES):
                lanes = slice(chunk * PART + tile * LANES, chunk * PART + (tile + 1) * LANES)
                held = []

                def emit(i, total):
                    part = slice(i * TILE, (i + 1) * TILE)
                    held.append(near[part, lanes] + gate_feat[part, lanes] * total)
                    if i % 2 == 1:
                        held_out[(i - 1) * TILE : (i + 1) * TILE, lanes] = jnp.concatenate(
                            held[-2:], 0
                        ).astype(BF16)

                response(*modal_tables(state, decays, leads, lanes), rows // TILE, emit)
            copy = pltpu.make_async_copy(held_out.at[:, here], out.at[:, here], sent.at[chunk])
            copy.start()
            copies.append(copy)
        for copy in copies:
            copy.wait()


SCALAR = pl.BlockSpec(memory_space=pltpu.SMEM)
KEPT = pl.BlockSpec(memory_space=pltpu.VMEM)
FAR = pl.BlockSpec(memory_space=pl.ANY)
MIB = 1024 * 1024


def call(kernel, name, in_specs, out_shape, scratch=(), flops=0, moved=0, room=12, out_specs=None, aliases=None):
    return pl.pallas_call(
        kernel,
        in_specs=in_specs,
        out_specs=out_specs or jax.tree.map(lambda _: KEPT, out_shape),
        out_shape=out_shape,
        scratch_shapes=list(scratch),
        input_output_aliases=aliases or {},
        compiler_params=pltpu.CompilerParams(vmem_limit_bytes=room * MIB),
        name=name,
        cost_estimate=pl.CostEstimate(flops=flops, bytes_accessed=moved, transcendentals=0),
    )


def in_hbm(value):
    return pltpu.with_memory_space_constraint(value, pltpu.HBM)


def arr(shape, dtype):
    return jax.ShapeDtypeStruct(shape, dtype)


def passed_along(value, axis, steps):
    count = lax.axis_size(axis)
    return lax.ppermute(value, axis, [(source, source + steps) for source in range(count - steps)])


def exchanged(value, axis, flip):
    count = lax.axis_size(axis)
    return lax.ppermute(value, axis, [(source, source ^ flip) for source in range(count)])


def sum_over(value, axis):
    total = value
    for part in [exchanged(value, axis, turn) for turn in range(1, lax.axis_size(axis))]:
        total = total + part
    return total


def stages(count):
    group = 1
    while group < count:
        radix = 4 if count // group >= 4 else 2
        yield group, radix
        group *= radix


def carry_weights(place, count, row_count, rates):
    for group, radix in stages(count):
        digit = (place // group) % radix
        within = (place % group).astype(F32)
        for turn in range(radix):
            member = digit ^ turn
            behind = (digit - 1 - member).astype(F32) * group + within
            decay = jnp.exp(-rates * (row_count * jnp.maximum(behind, 0.0)))
            yield jnp.where(member < digit, decay, 0.0)
            left = ((radix - 1 - member) * group).astype(F32)
            yield jnp.exp(-rates * (row_count * left))


def carried_state(state, weights, beside):
    count = lax.axis_size("ctx")
    known = incoming = jnp.zeros_like(state)
    sent = state
    at = 0
    for group, radix in stages(count):
        known = known + incoming
        if group > 1 and group * radix == count:
            state = state + beside
        sent = state.astype(BF16)
        got = [state]
        for turn in range(1, radix):
            got.append(exchanged(sent, "ctx", turn * group).astype(F32))
        incoming = sum(weights[at + 2 * turn] * got[turn] for turn in range(radix))
        state = sum(weights[at + 2 * turn + 1] * got[turn] for turn in range(radix))
        at += 2 * radix
    return known, incoming, sent


def body(
    gate_medium,
    key_medium,
    value_medium,
    short_medium,
    filter_medium,
    skip_medium,
    norm_gain,
    gate_long,
    key_long,
    short_long,
    decay_rates,
    residues,
    skip_long,
):
    rows, width = gate_medium.shape
    modes = decay_rates.shape[0]
    blocks = rows // BLOCK
    count = lax.axis_size("ctx")
    all_width = width * lax.axis_size("ch")
    exact_rows, split_rows, backward, backward_late = (jnp.asarray(m) for m in transforms())
    far = [
        in_hbm(value)
        for value in (key_medium, value_medium, gate_medium, gate_long, key_long, short_medium)
    ]
    place = lax.axis_index("ctx").astype(jnp.int32).reshape(1)
    pack = call(
        pack_kernel, "pack", [SCALAR] + [FAR] * 6, arr((EARLY, width), BF16),
        [
            pltpu.VMEM((2, EARLY, width), BF16), pltpu.VMEM((3, RIM, width), BF16),
            pltpu.VMEM((2, 3, width), F32), pltpu.SemaphoreType.DMA((width // WIDTH, 6)),
        ],
    )(place, *far)
    halo = passed_along(pack, "ctx", 1)

    skip_row = skip_medium[None]
    mode_weight = residues * jnp.sqrt(-jnp.expm1(-2.0 * decay_rates))
    turns = sum(2 * radix for _, radix in stages(count)) or 1
    conv_early, gate_early, mixed_late, squares_late, taps_hat, heads = call(
        own_kernel, "own", [KEPT] * 10,
        [
            arr((EARLY, width), F32), arr((EARLY, width), F32),
            arr((rows - EARLY, width), BF16), arr((TILE, rows - EARLY), F32),
            arr((2 * BLOCK, width), F32), arr((4 * TILE, width), F32),
        ],
        [pltpu.VMEM((rows - EARLY, LANES), F32)],
        flops=2000 * rows * width, moved=10 * rows * width, room=16,
    )(
        gate_medium, key_medium, value_medium, short_medium, skip_row, filter_medium, split_rows,
        exact_rows, backward, pack,
    )

    table = arr((modes, TILE, width), F32)
    long_hat, carry, leads, decays, tails = call(
        lambda *refs: impulse_kernel(count, *refs), "impulse",
        [SCALAR] + [KEPT] * 4,
        [
            arr((blocks, 2 * BLOCK, width), F32), arr((turns, modes, width), F32),
            table, table, table,
        ],
        [pltpu.VMEM((rows, WIDTH), F32)],
        flops=2000 * rows * width, moved=10 * rows * width,
    )(place, decay_rates, mode_weight, exact_rows, squares_late)

    total_late = sum_over(squares_late, "ch")
    product_late, state_late = call(
        lambda *refs: late_kernel(all_width, *refs), "late", [KEPT] * 7,
        [arr((rows - TURN, width), BF16), arr((modes, width), F32)],
        flops=100 * rows * width, moved=10 * rows * width,
    )(total_late, mixed_late, key_long, norm_gain[None], short_long, decays, tails)

    mixed_medium, mixed_rim, squares, rim_long = call(
        medium_kernel, "medium", [KEPT] * 12,
        [
            arr((rows, width), BF16), arr((TILE, width), F32), arr((TILE, EARLY + TILE), F32),
            arr((TILE, width), F32),
        ],
        [pltpu.VMEM((EARLY + TILE, LANES), F32)],
        flops=1000 * rows * width, moved=10 * rows * width,
    )(
        halo, heads, short_medium, skip_row, taps_hat, exact_rows, backward_late,
        conv_early, gate_early, mixed_late, state_late, carry,
    )

    total_squares = sum_over(squares, "ch")
    long_parts, tails_far = call(
        value_kernel, "value", [KEPT] * 8, [arr((3, TURN, width), F32), table],
        flops=1000 * rows * width, moved=10 * rows * width,
    )(
        mixed_medium, mixed_rim, norm_gain[None], key_long, rim_long, short_long, decay_rates, tails
    )
    product_early, state = call(
        lambda *refs: state_kernel(all_width, *refs), "state", [KEPT] * 6,
        [arr((TURN, width), BF16), arr((modes, width), F32)],
        [pltpu.VMEM((3, TURN, LANES), F32)],
        flops=100 * rows * width, moved=10 * rows * width,
    )(total_squares, total_late, long_parts, tails_far, decays, state_late)

    local, done = call(
        local_kernel, "local", [KEPT] * 6, [arr((rows, width), F32), arr((1, width), F32)],
        flops=2000 * rows * width, moved=14 * rows * width,
    )(product_early, product_late, long_hat, skip_long[None], exact_rows, backward)
    known, incoming, last_sent = carried_state(state, carry, done)
    near, gate_feat, mixed_out, mixed_long = call(
        near_kernel, "near", [KEPT] * 9,
        [
            arr((rows, width), F32), arr((rows, width), F32), arr((rows, width), BF16),
            arr((rows, width), BF16),
        ],
        [pltpu.VMEM((rows, width), BF16), pltpu.SemaphoreType.DMA((width // WIDTH + 1,))],
        out_specs=[KEPT, KEPT, FAR, FAR],
        flops=1000 * rows * width, moved=14 * rows * width,
    )(known, decays, leads, local, gate_long, rim_long, short_long, mixed_medium, last_sent)
    mixed_long = call(
        lambda *refs: finish_kernel(count, *refs), "finish", [SCALAR] + [KEPT] * 5 + [FAR],
        arr((rows, width), BF16),
        [pltpu.VMEM((rows, width), BF16), pltpu.SemaphoreType.DMA((width // PART,))],
        out_specs=FAR, aliases={6: 0},
        flops=100 * rows * width, moved=8 * rows * width,
    )(place, incoming, decays, leads, near, gate_feat, mixed_long)
    return (mixed_out, mixed_long)


def solution(mesh):
    placed = (
        P("ctx", "ch"),
        P("ctx", "ch"),
        P("ctx", "ch"),
        P(None, None, "ch"),
        P(None, "ch"),
        P("ch"),
        P("ch"),
        P("ctx", "ch"),
        P("ctx", "ch"),
        P(None, None, "ch"),
        P(None, "ch"),
        P(None, "ch"),
        P("ch"),
    )
    return jax.shard_map(
        body,
        mesh=mesh,
        in_specs=placed,
        out_specs=(P("ctx", "ch"), P("ctx", "ch")),
        check_vma=False,
    )
```

```python
import jax
import jax.numpy as jnp
import ml_dtypes
import numpy as np
from jax import lax
from jax.experimental import pallas as pl
from jax.experimental.pallas import tpu as pltpu
from jax.sharding import PartitionSpec as P

F32 = jnp.float32
BF16 = jnp.bfloat16
BLOCK = 128
HALF = BLOCK // 2
TILE = 8
LANES = 128
WIDTH = 1024
PART = 512


RIM = 2 * TILE
EARLY = BLOCK + RIM
TURN = EARLY + RIM


def split_np(values):
    high = values.astype(ml_dtypes.bfloat16)
    low = (values - high.astype(np.float64)).astype(ml_dtypes.bfloat16)
    return high, low


def angles(times):
    order = np.concatenate([np.arange(0, BLOCK, 2), np.arange(1, BLOCK, 2)])
    return np.pi * (order[:, None] + 0.5) * times[None, :] / BLOCK


def transforms():
    angle = angles(np.arange(BLOCK))
    forward = np.concatenate([np.cos(angle), -np.sin(angle)], 0)
    high, low = split_np(forward)
    exact_rows = np.concatenate([high, low], 1)
    split_rows = np.concatenate([high, high, low], 1)
    backward = np.concatenate(split_np(forward.T / BLOCK), 0)
    times = np.arange(-RIM, EARLY) + BLOCK - 2
    angle = angles(times)
    late = np.concatenate([np.cos(angle), -np.sin(angle)], 0).T / BLOCK
    late = late * ((times >= BLOCK - 4) & (times < 2 * BLOCK - 1))[:, None]
    return exact_rows, split_rows, backward, np.concatenate(split_np(late), 0)


def dot(a, b):
    return jnp.dot(a, b, preferred_element_type=F32)


def split(values):
    high = values.astype(BF16)
    return high, (values - high.astype(F32)).astype(BF16)


def forward_exact(matrix, block):
    return dot(matrix, jnp.concatenate([block, block], 0))


def forward_split(matrix, block):
    high, low = split(block)
    return dot(matrix, jnp.concatenate([high, low, high], 0))


def backward_exact(matrix, spectrum):
    rows = matrix.shape[0] // 2
    both = dot(matrix, spectrum.astype(BF16))
    return both[:rows] + both[rows:]


def turned(spectrum):
    even_re, odd_re, even_im, odd_im = (spectrum[i * HALF : (i + 1) * HALF] for i in range(4))
    return jnp.concatenate([-even_im, odd_im, even_re, -odd_re], 0)


def times(a, b):
    a_re, a_im, b_re, b_im = a[:BLOCK], a[BLOCK:], b[:BLOCK], b[BLOCK:]
    return jnp.concatenate([a_re * b_re - a_im * b_im, a_re * b_im + a_im * b_re], 0)


def shifted_filter(frame, weights):
    return (
        weights[0:1] * frame
        + weights[1:2] * pltpu.roll(frame, 1, 0)
        + weights[2:3] * pltpu.roll(frame, 2, 0)
    )


def ahead_filter(frame, weights):
    rows = frame.shape[0]
    return (
        weights[0:1] * pltpu.roll(frame, rows - 2, 0)
        + weights[1:2] * pltpu.roll(frame, rows - 1, 0)
        + weights[2:3] * frame
    )


def rows_of(shape):
    return lax.broadcasted_iota(jnp.int32, shape, 0)


def over_channels(width, step, unrolled=False):
    if unrolled:
        for i in range(width // WIDTH):
            step(pl.ds(i * WIDTH, WIDTH), i * WIDTH)
        return

    def one(i, _):
        step(pl.ds(pl.multiple_of(i * WIDTH, WIDTH), WIDTH), i * WIDTH)
        return 0

    lax.fori_loop(0, width // WIDTH, one, 0)


def sublane_sum(values):
    return jnp.sum(values, axis=0, keepdims=True)


def lane_parts(values):
    total = values[:, :LANES]
    for tile in range(1, values.shape[1] // LANES):
        total = total + values[:, tile * LANES : (tile + 1) * LANES]
    return total


def row_sums(partial):
    return lax.dot_general(
        jnp.ones((TILE, LANES), F32),
        partial,
        (((1,), (1,)), ((), ())),
        precision=lax.Precision.HIGHEST,
        preferred_element_type=F32,
    )


def norm_factors(squares, all_width):
    factor = lax.rsqrt(squares / all_width + 1e-06)
    high, rest = split(factor)
    low = (factor - high.astype(F32) - rest.astype(F32)).astype(BF16)
    row = rows_of(factor.shape)
    stack = jnp.where(row == 0, high.astype(F32), jnp.where(row == 1, rest.astype(F32), 0.0))
    stack = jnp.where(row == 2, low.astype(F32), stack)
    stack = jnp.concatenate([stack, jnp.zeros_like(stack)], 0).astype(BF16)
    return lax.dot_general(
        stack,
        jnp.ones((RIM, LANES), BF16),
        (((0,), (0,)), ((), ())),
        preferred_element_type=F32,
    )


def pack_kernel(
    _, key, value, gate, gate_long, key_long, short, out, tops, ends, taps, arrived
):
    rows, width = key.shape
    copies = []
    for chunk in range(width // WIDTH):
        here = pl.ds(chunk * WIDTH, WIDTH)
        pairs = [(short.at[1:3, :, here], taps.at[:, :, here])]
        for i, ref in enumerate((key, value)):
            pairs.append((ref.at[rows - EARLY :, here], tops.at[i, :, here]))
        for i, ref in enumerate((gate, gate_long, key_long)):
            pairs.append((ref.at[rows - RIM :, here], ends.at[i, :, here]))
        copies.append(
            [
                pltpu.make_async_copy(source, target, arrived.at[chunk, i])
                for i, (source, target) in enumerate(pairs)
            ]
        )
    for group in copies:
        for copy in group:
            copy.start()
    for chunk in range(width // WIDTH):
        here = pl.ds(chunk * WIDTH, WIDTH)
        for copy in copies[chunk]:
            copy.wait()
        for lanes in lane_tiles(chunk * WIDTH):
            key_part, value_part = tops[0, :, lanes].astype(F32), tops[1, :, lanes].astype(F32)
            product = ahead_filter(key_part, taps[0, :, lanes]) * ahead_filter(
                value_part, taps[1, :, lanes]
            )
            row = rows_of((TILE, LANES))
            gate_end, gate_long_end, key_long_end = (
                ends[i, :, lanes].astype(F32)[TILE:] for i in range(3)
            )
            first = jnp.where(
                row < 2,
                pltpu.roll(key_part[-TILE:], 2, 0),
                jnp.where(row < 4, pltpu.roll(value_part[-TILE:], 4, 0), gate_end),
            )
            second = jnp.where(
                row < 2,
                pltpu.roll(gate_long_end, 2, 0),
                jnp.where(row < 4, pltpu.roll(key_long_end, 4, 0), product[TILE:RIM]),
            )
            out[:, lanes] = jnp.concatenate([first, second, product[RIM:]], 0).astype(BF16)


def mode_tables(rates, mode, lanes, offset, sign):
    rate = jnp.broadcast_to(rates[mode : mode + 1, lanes], (TILE, LANES))
    row = rows_of((TILE, LANES)).astype(F32)
    return jnp.exp(-rate * (offset + sign * row)), jnp.exp(-TILE * rate)


def response(starts, steps, count, emit):
    parts = list(starts)
    for i in range(count):
        level = parts
        while len(level) > 1:
            level = [a + b for a, b in zip(level[::2], level[1::2])]
        emit(i, level[0])
        if i + 1 < count:
            parts = [part * step for part, step in zip(parts, steps)]


def lane_tiles(base):
    starts = [base + tile * LANES for tile in range(WIDTH // LANES)]
    if isinstance(base, int):
        return [pl.ds(start, LANES) for start in starts]
    return [pl.ds(pl.multiple_of(start, LANES), LANES) for start in starts]


def impulse_kernel(
    count, place, rates, weights, exact_rows, _, long_hat, carry, leads, decays, tails, impulse
):
    modes, width = rates.shape
    rows = impulse.shape[0]
    for i, weight in enumerate(carry_weights(place[0], count, rows, rates[...])):
        carry[i] = weight

    def step(here, base):
        for tile, lanes in enumerate(lane_tiles(base)):
            starts, steps = [], []
            for mode in range(modes):
                lead, decay = mode_tables(rates, mode, lanes, 0.0, 1.0)
                start = lead * weights[mode : mode + 1, lanes]
                leads[mode, :, lanes] = start * jnp.exp(-rates[mode : mode + 1, lanes])
                decays[mode, :, lanes] = decay
                tails[mode, :, lanes] = mode_tables(rates, mode, lanes, TILE - 1.0, -1.0)[0]
                starts.append(start)
                steps.append(decay)

            def emit(i, total):
                impulse[i * TILE : (i + 1) * TILE, tile * LANES : (tile + 1) * LANES] = total

            response(starts, steps, rows // TILE, emit)
        for block in range(rows // BLOCK):
            long_hat[block, :, here] = forward_exact(
                exact_rows[...], impulse[block * BLOCK : (block + 1) * BLOCK].astype(BF16)
            )
        for block in reversed(range(1, rows // BLOCK)):
            long_hat[block, :, here] = long_hat[block, :, here] + turned(
                long_hat[block - 1, :, here]
            )

    over_channels(width, step)


def own_kernel(
    gate, key, value, short, skip, taps, split_rows, exact_rows, backward, _,
    conv_early, gate_early, mixed_late, squares_late, taps_hat, heads, sums,
):
    rows, width = gate.shape
    sums[...] = jnp.zeros(sums.shape, F32)

    def step(here, base):
        hat = forward_split(split_rows[...], taps[:, here])
        taps_hat[:, here] = hat
        keys, values, gates = (ref[:, here].astype(F32) for ref in (key, value, gate))
        heads[:, here] = jnp.concatenate(
            [part[:TILE] for part in (keys, values, gates)]
            + [taps[BLOCK - TILE :, here]],
            0,
        )
        product = shifted_filter(keys, short[1, :, here]) * shifted_filter(
            values, short[2, :, here]
        )
        row = rows_of((TILE, WIDTH))
        product = jnp.concatenate(
            [jnp.where(row < 2, 0.0, product[:TILE]), product[TILE:]], 0
        ).astype(BF16)
        before = None
        conv = []
        for block in range(rows // BLOCK):
            now = forward_exact(exact_rows[...], product[block * BLOCK : (block + 1) * BLOCK])
            window = now if before is None else now + turned(before)
            conv.append(backward_exact(backward[...], times(hat, window)))
            before = now
        total = jnp.concatenate(conv, 0) + skip[:, here] * product.astype(F32)
        feat = shifted_filter(gates, short[0, :, here])
        conv_early[:, here] = total[:EARLY]
        gate_early[:, here] = feat[:EARLY]
        mixed = (feat[EARLY:] * total[EARLY:]).astype(BF16)
        mixed_late[:, here] = mixed
        kept = mixed.astype(F32)
        sums[...] = sums[...] + lane_parts(kept * kept)

    over_channels(width, step)
    squares_late[...] = row_sums(sums[...])


def medium_kernel(
    halo, heads, short, skip, taps_hat, exact_rows, backward,
    conv_early, gate_early, mixed_late, _, __,
    mixed, mixed_rim, squares, rim_long, total,
):
    width = halo.shape[1]
    total[...] = jnp.zeros(total.shape, F32)

    def step(here, base):
        halo_part = halo[:, here].astype(F32)
        rim, rim_late = halo_part[:TILE], halo_part[TILE:RIM]
        rim_long[:, here] = rim_late
        row = rows_of((TILE, WIDTH))
        key_part, value_part, gate_part, tail = (
            heads[i * TILE : (i + 1) * TILE, here] for i in range(4)
        )
        keys = jnp.where(row >= 6, pltpu.roll(key_part, 6, 0), pltpu.roll(rim, 4, 0))
        values = jnp.where(row >= 6, pltpu.roll(value_part, 6, 0), pltpu.roll(rim, 2, 0))
        start = shifted_filter(keys, short[1, :, here]) * shifted_filter(values, short[2, :, here])
        start = start.astype(BF16).astype(F32)
        end = jnp.where(row >= 6, start, halo_part[-TILE:])
        window = jnp.concatenate([halo_part[RIM:-TILE], end], 0).astype(BF16)
        spectrum = times(taps_hat[:, here], forward_exact(exact_rows[...], window))
        late = backward_exact(backward[...], spectrum)
        tap_a, tap_b, tap_c = (tail[i : i + 1] for i in (7, 6, 5))
        far_a, far_b, far_c = (rim_late[i : i + 1] for i in (5, 6, 7))
        skip_part = skip[:, here]
        rim_conv = late[TILE:RIM] + skip_part * pltpu.roll(end, 2, 0)
        rim_conv = rim_conv + jnp.where(
            row == 6, tap_a * far_a + tap_b * far_b + tap_c * far_c, tap_a * far_b + tap_b * far_c
        )
        rim_conv = jnp.where(row >= 6, rim_conv, 0.0)
        early = conv_early[:, here] + late[RIM:]
        extra = skip_part * jnp.where(row < 2, pltpu.roll(start, 2, 0), 0.0)
        extra = extra + jnp.where(row == 0, tap_a * far_c, 0.0)
        gates = shifted_filter(jnp.concatenate([rim, gate_part], 0), short[0, :, here])
        conv = jnp.concatenate([rim_conv, early[:TILE] + extra, early[TILE:]], 0)
        feat = jnp.concatenate([gates, gate_early[TILE:, here]], 0)
        kept = (feat * conv).astype(BF16).astype(F32)
        mixed[:EARLY, here] = kept[TILE:].astype(BF16)
        mixed[EARLY:, here] = mixed_late[:, here]
        mixed_rim[:, here] = kept[:TILE]
        total[...] = total[...] + lane_parts(kept * kept)

    over_channels(width, step, unrolled=True)
    squares[...] = row_sums(total[...])


def late_kernel(
    all_width, squares, mixed_late, key_long, gain, short, decays, tails,
    product_out, state, late_factors,
):
    rows, width = key_long.shape
    modes = decays.shape[0]
    factors = norm_factors(squares[...], all_width)
    late_factors[...] = factors

    def step(here, base):
        for lanes in lane_tiles(base):
            frame = mixed_late[:, lanes].astype(F32) * factors
            feat = shifted_filter(frame, short[2, :, lanes] * gain[:, lanes])
            keys = shifted_filter(key_long[EARLY:, lanes].astype(F32), short[1, :, lanes])
            product = (keys * feat)[TURN - EARLY :]
            product_out[:, lanes] = product.astype(BF16)
            held = [product[:TILE]] * modes
            steps = [decays[mode, :, lanes] for mode in range(modes)]
            for i in range(TILE, rows - TURN, TILE):
                held = [old * decay + product[i : i + TILE] for old, decay in zip(held, steps)]
            for mode in range(modes):
                state[mode : mode + 1, lanes] = sublane_sum(held[mode] * tails[mode, :, lanes])

    over_channels(width, step, unrolled=True)


def value_kernel(
    mixed, mixed_rim, gain, key_long, gate_long, rim_long, short, rates, tails,
    parts, tails_far, gate_feat,
):
    rows, width = mixed.shape
    modes = rates.shape[0]

    def step(here, base):
        frame = jnp.concatenate([mixed_rim[:, here], mixed[:TURN, here].astype(F32)], 0)
        keys = shifted_filter(
            jnp.concatenate(
                [pltpu.roll(rim_long[:, here], 4, 0), key_long[:TURN, here].astype(F32)], 0
            ),
            short[1, :, here],
        )[TILE:]
        gates = jnp.concatenate(
            [pltpu.roll(rim_long[:, here], 6, 0), gate_long[:, here].astype(F32)], 0
        )
        gate_feat[:, here] = shifted_filter(gates, short[0, :, here])[TILE:]
        weights = short[2, :, here] * gain[:, here]
        for j in range(3):
            moved = frame if j == 0 else pltpu.roll(frame, j, 0)
            parts[j, :, here] = keys * (weights[j : j + 1] * moved[TILE:])
        for mode in range(modes):
            tails_far[mode, :, here] = tails[mode, :, here] * jnp.exp(
                (TURN - rows) * rates[mode : mode + 1, here]
            )

    over_channels(width, step, unrolled=True)


def state_kernel(
    all_width, squares, late_factors, parts, tails_far, decays, state_late,
    product_out, state, factors,
):
    width = product_out.shape[1]
    modes = decays.shape[0]
    inverse = norm_factors(squares[...], all_width)
    inverse = jnp.concatenate(
        [inverse, late_factors[: TURN - EARLY]], 0
    )
    factors[0] = inverse[TILE:]
    factors[1] = pltpu.roll(inverse, 1, 0)[TILE:]
    factors[2] = pltpu.roll(inverse, 2, 0)[TILE:]

    def step(here, base):
        for lanes in lane_tiles(base):
            steps = [decays[mode, :, lanes] for mode in range(modes)]
            held = None
            for i in range(0, TURN, 2 * TILE):
                part = slice(i, i + 2 * TILE)
                product = (
                    parts[0, part, lanes] * factors[0, part]
                    + parts[1, part, lanes] * factors[1, part]
                    + parts[2, part, lanes] * factors[2, part]
                )
                product_out[part, lanes] = product.astype(BF16)
                for piece in (product[:TILE], product[TILE:]):
                    if held is None:
                        held = [piece] * modes
                    else:
                        held = [old * decay + piece for old, decay in zip(held, steps)]
            for mode in range(modes):
                state[mode : mode + 1, lanes] = state_late[mode : mode + 1, lanes] + sublane_sum(
                    held[mode] * tails_far[mode, :, lanes]
                )

    over_channels(width, step, unrolled=True)


def local_kernel(early, late, long_hat, skip, exact_rows, backward, out, done):
    rows, width = out.shape
    done[...] = jnp.zeros(done.shape, F32)

    def step(here, base):
        spectra = []
        product = jnp.concatenate([early[:, here].astype(F32), late[:, here].astype(F32)], 0)
        for block in range(rows // BLOCK):
            part = slice(block * BLOCK, (block + 1) * BLOCK)
            piece = product[part]
            spectra.append(forward_exact(exact_rows[...], piece.astype(BF16)))
            total = times(long_hat[0, :, here], spectra[block])
            for lag in range(1, block + 1):
                total = total + times(long_hat[lag, :, here], spectra[block - lag])
            out[part, here] = backward_exact(backward[...], total) + skip[:, here] * piece

    over_channels(width, step, unrolled=True)


def modal_tables(state, decays, leads, lanes):
    modes = decays.shape[0]
    starts = [leads[mode, :, lanes] * state[mode : mode + 1, lanes] for mode in range(modes)]
    return starts, [decays[mode, :, lanes] for mode in range(modes)]


def near_kernel(
    state, decays, leads, local, gate_feat, mixed, _,
    near, mixed_out, out, held_out, sent,
):
    rows, width = local.shape
    copies = [pltpu.make_async_copy(mixed, mixed_out, sent.at[width // WIDTH])]
    copies[0].start()

    def step(here, base):
        for lanes in lane_tiles(base):

            held = []

            def emit(i, total):
                part = slice(i * TILE, (i + 1) * TILE)
                held.append(gate_feat[part, lanes] * (local[part, lanes] + total))
                near[part, lanes] = held[-1]
                if i % 2 == 1:
                    held_out[(i - 1) * TILE : (i + 1) * TILE, lanes] = jnp.concatenate(
                        held[-2:], 0
                    ).astype(BF16)

            response(*modal_tables(state, decays, leads, lanes), rows // TILE, emit)
        copy = pltpu.make_async_copy(
            held_out.at[:, here], out.at[:, here], sent.at[base // WIDTH]
        )
        copy.start()
        copies.append(copy)

    over_channels(width, step, unrolled=True)
    for copy in copies:
        copy.wait()


def finish_kernel(count, place, state, decays, leads, near, gate_feat, _, out, held_out, sent):
    rows, width = near.shape
    group, radix = list(stages(count))[-1] if count > 1 else (1, 1)

    @pl.when((place[0] // group) % radix > 0)
    def _():
        copies = []
        for chunk in range(width // PART):
            here = pl.ds(chunk * PART, PART)
            for tile in range(PART // LANES):
                lanes = slice(chunk * PART + tile * LANES, chunk * PART + (tile + 1) * LANES)
                held = []

                def emit(i, total):
                    part = slice(i * TILE, (i + 1) * TILE)
                    held.append(near[part, lanes] + gate_feat[part, lanes] * total)
                    if i % 2 == 1:
                        held_out[(i - 1) * TILE : (i + 1) * TILE, lanes] = jnp.concatenate(
                            held[-2:], 0
                        ).astype(BF16)

                response(*modal_tables(state, decays, leads, lanes), rows // TILE, emit)
            copy = pltpu.make_async_copy(held_out.at[:, here], out.at[:, here], sent.at[chunk])
            copy.start()
            copies.append(copy)
        for copy in copies:
            copy.wait()


SCALAR = pl.BlockSpec(memory_space=pltpu.SMEM)
KEPT = pl.BlockSpec(memory_space=pltpu.VMEM)
FAR = pl.BlockSpec(memory_space=pl.ANY)
MIB = 1024 * 1024


def call(kernel, name, in_specs, out_shape, scratch=(), flops=0, moved=0, room=12, out_specs=None, aliases=None):
    return pl.pallas_call(
        kernel,
        in_specs=in_specs,
        out_specs=out_specs or jax.tree.map(lambda _: KEPT, out_shape),
        out_shape=out_shape,
        scratch_shapes=list(scratch),
        input_output_aliases=aliases or {},
        compiler_params=pltpu.CompilerParams(vmem_limit_bytes=room * MIB),
        name=name,
        cost_estimate=pl.CostEstimate(flops=flops, bytes_accessed=moved, transcendentals=0),
    )


def in_hbm(value):
    return pltpu.with_memory_space_constraint(value, pltpu.HBM)


def arr(shape, dtype):
    return jax.ShapeDtypeStruct(shape, dtype)


def passed_along(value, axis, steps):
    count = lax.axis_size(axis)
    return lax.ppermute(value, axis, [(source, source + steps) for source in range(count - steps)])


def exchanged(value, axis, flip):
    count = lax.axis_size(axis)
    return lax.ppermute(value, axis, [(source, source ^ flip) for source in range(count)])


def sum_over(value, axis):
    total = value
    for part in [exchanged(value, axis, turn) for turn in range(1, lax.axis_size(axis))]:
        total = total + part
    return total


def stages(count):
    group = 1
    while group < count:
        radix = 4 if count // group >= 4 else 2
        yield group, radix
        group *= radix


def carry_weights(place, count, row_count, rates):
    for group, radix in stages(count):
        digit = (place // group) % radix
        within = (place % group).astype(F32)
        for turn in range(radix):
            member = digit ^ turn
            behind = (digit - 1 - member).astype(F32) * group + within
            decay = jnp.exp(-rates * (row_count * jnp.maximum(behind, 0.0)))
            yield jnp.where(member < digit, decay, 0.0)
            left = ((radix - 1 - member) * group).astype(F32)
            yield jnp.exp(-rates * (row_count * left))


def carried_state(state, weights, beside):
    count = lax.axis_size("ctx")
    known = incoming = jnp.zeros_like(state)
    sent = state
    at = 0
    for group, radix in stages(count):
        known = known + incoming
        if group > 1 and group * radix == count:
            state = state + beside
        sent = state.astype(BF16)
        got = [state]
        for turn in range(1, radix):
            got.append(exchanged(sent, "ctx", turn * group).astype(F32))
        incoming = sum(weights[at + 2 * turn] * got[turn] for turn in range(radix))
        state = sum(weights[at + 2 * turn + 1] * got[turn] for turn in range(radix))
        at += 2 * radix
    return known, incoming, sent


def body(
    gate_medium,
    key_medium,
    value_medium,
    short_medium,
    filter_medium,
    skip_medium,
    norm_gain,
    gate_long,
    key_long,
    short_long,
    decay_rates,
    residues,
    skip_long,
):
    rows, width = gate_medium.shape
    modes = decay_rates.shape[0]
    blocks = rows // BLOCK
    count = lax.axis_size("ctx")
    all_width = width * lax.axis_size("ch")
    exact_rows, split_rows, backward, backward_late = (jnp.asarray(m) for m in transforms())
    far = [
        in_hbm(value)
        for value in (key_medium, value_medium, gate_medium, gate_long, key_long, short_medium)
    ]
    place = lax.axis_index("ctx").astype(jnp.int32).reshape(1)
    pack = call(
        pack_kernel, "pack", [SCALAR] + [FAR] * 6, arr((EARLY, width), BF16),
        [
            pltpu.VMEM((2, EARLY, width), BF16), pltpu.VMEM((3, RIM, width), BF16),
            pltpu.VMEM((2, 3, width), F32), pltpu.SemaphoreType.DMA((width // WIDTH, 6)),
        ],
    )(place, *far)
    halo = passed_along(pack, "ctx", 1)

    skip_row = skip_medium[None]
    mode_weight = residues * jnp.sqrt(-jnp.expm1(-2.0 * decay_rates))
    turns = sum(2 * radix for _, radix in stages(count)) or 1
    conv_early, gate_early, mixed_late, squares_late, taps_hat, heads = call(
        own_kernel, "own", [KEPT] * 10,
        [
            arr((EARLY, width), F32), arr((EARLY, width), F32),
            arr((rows - EARLY, width), BF16), arr((TILE, rows - EARLY), F32),
            arr((2 * BLOCK, width), F32), arr((4 * TILE, width), F32),
        ],
        [pltpu.VMEM((rows - EARLY, LANES), F32)],
        flops=2000 * rows * width, moved=10 * rows * width, room=16,
    )(
        gate_medium, key_medium, value_medium, short_medium, skip_row, filter_medium, split_rows,
        exact_rows, backward, pack,
    )

    table = arr((modes, TILE, width), F32)
    long_hat, carry, leads, decays, tails = call(
        lambda *refs: impulse_kernel(count, *refs), "impulse",
        [SCALAR] + [KEPT] * 4,
        [
            arr((blocks, 2 * BLOCK, width), F32), arr((turns, modes, width), F32),
            table, table, table,
        ],
        [pltpu.VMEM((rows, WIDTH), F32)],
        flops=2000 * rows * width, moved=10 * rows * width,
    )(place, decay_rates, mode_weight, exact_rows, squares_late)

    total_late = sum_over(squares_late, "ch")
    product_late, state_late, late_factors = call(
        lambda *refs: late_kernel(all_width, *refs), "late", [KEPT] * 7,
        [
            arr((rows - TURN, width), BF16), arr((modes, width), F32),
            arr((rows - EARLY, LANES), F32),
        ],
        flops=100 * rows * width, moved=10 * rows * width,
    )(total_late, mixed_late, key_long, norm_gain[None], short_long, decays, tails)

    mixed_medium, mixed_rim, squares, rim_long = call(
        medium_kernel, "medium", [KEPT] * 12,
        [
            arr((rows, width), BF16), arr((TILE, width), F32), arr((TILE, EARLY + TILE), F32),
            arr((TILE, width), F32),
        ],
        [pltpu.VMEM((EARLY + TILE, LANES), F32)],
        flops=1000 * rows * width, moved=10 * rows * width,
    )(
        halo, heads, short_medium, skip_row, taps_hat, exact_rows, backward_late,
        conv_early, gate_early, mixed_late, state_late, carry,
    )

    total_squares = sum_over(squares, "ch")
    long_parts, tails_far, gate_feat = call(
        value_kernel, "value", [KEPT] * 9,
        [arr((3, TURN, width), F32), table, arr((rows, width), F32)],
        flops=1000 * rows * width, moved=10 * rows * width,
    )(
        mixed_medium, mixed_rim, norm_gain[None], key_long, gate_long, rim_long, short_long,
        decay_rates, tails,
    )
    product_early, state = call(
        lambda *refs: state_kernel(all_width, *refs), "state", [KEPT] * 6,
        [arr((TURN, width), BF16), arr((modes, width), F32)],
        [pltpu.VMEM((3, TURN, LANES), F32)],
        flops=100 * rows * width, moved=10 * rows * width,
    )(total_squares, late_factors, long_parts, tails_far, decays, state_late)

    local, done = call(
        local_kernel, "local", [KEPT] * 6, [arr((rows, width), F32), arr((1, width), F32)],
        flops=2000 * rows * width, moved=14 * rows * width,
    )(product_early, product_late, long_hat, skip_long[None], exact_rows, backward)
    known, incoming, last_sent = carried_state(state, carry, done)
    near, mixed_out, mixed_long = call(
        near_kernel, "near", [KEPT] * 7,
        [
            arr((rows, width), F32), arr((rows, width), BF16), arr((rows, width), BF16),
        ],
        [pltpu.VMEM((rows, width), BF16), pltpu.SemaphoreType.DMA((width // WIDTH + 1,))],
        out_specs=[KEPT, FAR, FAR],
        flops=1000 * rows * width, moved=14 * rows * width,
    )(known, decays, leads, local, gate_feat, mixed_medium, last_sent)
    mixed_long = call(
        lambda *refs: finish_kernel(count, *refs), "finish", [SCALAR] + [KEPT] * 5 + [FAR],
        arr((rows, width), BF16),
        [pltpu.VMEM((rows, width), BF16), pltpu.SemaphoreType.DMA((width // PART,))],
        out_specs=FAR, aliases={6: 0},
        flops=100 * rows * width, moved=8 * rows * width,
    )(place, incoming, decays, leads, near, gate_feat, mixed_long)
    return (mixed_out, mixed_long)


def solution(mesh):
    placed = (
        P("ctx", "ch"),
        P("ctx", "ch"),
        P("ctx", "ch"),
        P(None, None, "ch"),
        P(None, "ch"),
        P("ch"),
        P("ch"),
        P("ctx", "ch"),
        P("ctx", "ch"),
        P(None, None, "ch"),
        P(None, "ch"),
        P(None, "ch"),
        P("ch"),
    )
    return jax.shard_map(
        body,
        mesh=mesh,
        in_specs=placed,
        out_specs=(P("ctx", "ch"), P("ctx", "ch")),
        check_vma=False,
    )
```

```python
import jax
import jax.numpy as jnp
import ml_dtypes
import numpy as np
from jax import lax
from jax.experimental import pallas as pl
from jax.experimental.pallas import tpu as pltpu
from jax.sharding import PartitionSpec as P

F32 = jnp.float32
BF16 = jnp.bfloat16
BLOCK = 128
HALF = BLOCK // 2
TILE = 8
LANES = 128
WIDTH = 1024
PART = 512


RIM = 2 * TILE
EARLY = BLOCK + RIM
TURN = EARLY + RIM


def split_np(values):
    high = values.astype(ml_dtypes.bfloat16)
    low = (values - high.astype(np.float64)).astype(ml_dtypes.bfloat16)
    return high, low


def angles(times):
    order = np.concatenate([np.arange(0, BLOCK, 2), np.arange(1, BLOCK, 2)])
    return np.pi * (order[:, None] + 0.5) * times[None, :] / BLOCK


def transforms():
    angle = angles(np.arange(BLOCK))
    forward = np.concatenate([np.cos(angle), -np.sin(angle)], 0)
    high, low = split_np(forward)
    exact_rows = np.concatenate([high, low], 1)
    split_rows = np.concatenate([high, high, low], 1)
    backward = np.concatenate(split_np(forward.T / BLOCK), 0)
    times = np.arange(-RIM, EARLY) + BLOCK - 2
    angle = angles(times)
    late = np.concatenate([np.cos(angle), -np.sin(angle)], 0).T / BLOCK
    late = late * ((times >= BLOCK - 4) & (times < 2 * BLOCK - 1))[:, None]
    return exact_rows, split_rows, backward, split_np(late)[0]


def dot(a, b):
    return jnp.dot(a, b, preferred_element_type=F32)


def split(values):
    high = values.astype(BF16)
    return high, (values - high.astype(F32)).astype(BF16)


def forward_exact(matrix, block):
    return dot(matrix, jnp.concatenate([block, block], 0))


def forward_split(matrix, block):
    high, low = split(block)
    return dot(matrix, jnp.concatenate([high, low, high], 0))


def backward_exact(matrix, spectrum):
    rows = matrix.shape[0] // 2
    both = dot(matrix, spectrum.astype(BF16))
    return both[:rows] + both[rows:]


def turned(spectrum):
    even_re, odd_re, even_im, odd_im = (spectrum[i * HALF : (i + 1) * HALF] for i in range(4))
    return jnp.concatenate([-even_im, odd_im, even_re, -odd_re], 0)


def times(a, b):
    a_re, a_im, b_re, b_im = a[:BLOCK], a[BLOCK:], b[:BLOCK], b[BLOCK:]
    return jnp.concatenate([a_re * b_re - a_im * b_im, a_re * b_im + a_im * b_re], 0)


def shifted_filter(frame, weights):
    return (
        weights[0:1] * frame
        + weights[1:2] * pltpu.roll(frame, 1, 0)
        + weights[2:3] * pltpu.roll(frame, 2, 0)
    )


def ahead_filter(frame, weights):
    rows = frame.shape[0]
    return (
        weights[0:1] * pltpu.roll(frame, rows - 2, 0)
        + weights[1:2] * pltpu.roll(frame, rows - 1, 0)
        + weights[2:3] * frame
    )


def rows_of(shape):
    return lax.broadcasted_iota(jnp.int32, shape, 0)


def over_channels(width, step, unrolled=False):
    if unrolled:
        for i in range(width // WIDTH):
            step(pl.ds(i * WIDTH, WIDTH), i * WIDTH)
        return

    def one(i, _):
        step(pl.ds(pl.multiple_of(i * WIDTH, WIDTH), WIDTH), i * WIDTH)
        return 0

    lax.fori_loop(0, width // WIDTH, one, 0)


def sublane_sum(values):
    return jnp.sum(values, axis=0, keepdims=True)


def lane_parts(values):
    total = values[:, :LANES]
    for tile in range(1, values.shape[1] // LANES):
        total = total + values[:, tile * LANES : (tile + 1) * LANES]
    return total


def row_sums(partial):
    return lax.dot_general(
        jnp.ones((TILE, LANES), F32),
        partial,
        (((1,), (1,)), ((), ())),
        precision=lax.Precision.HIGHEST,
        preferred_element_type=F32,
    )


def norm_factors(squares, all_width):
    factor = lax.rsqrt(squares / all_width + 1e-06)
    high, rest = split(factor)
    low = (factor - high.astype(F32) - rest.astype(F32)).astype(BF16)
    row = rows_of(factor.shape)
    stack = jnp.where(row == 0, high.astype(F32), jnp.where(row == 1, rest.astype(F32), 0.0))
    stack = jnp.where(row == 2, low.astype(F32), stack)
    stack = jnp.concatenate([stack, jnp.zeros_like(stack)], 0).astype(BF16)
    return lax.dot_general(
        stack,
        jnp.ones((RIM, LANES), BF16),
        (((0,), (0,)), ((), ())),
        preferred_element_type=F32,
    )


def pack_kernel(
    _, key, value, gate, gate_long, key_long, short, out, tops, ends, taps, arrived
):
    rows, width = key.shape
    copies = []
    for chunk in range(width // WIDTH):
        here = pl.ds(chunk * WIDTH, WIDTH)
        pairs = [(short.at[1:3, :, here], taps.at[:, :, here])]
        for i, ref in enumerate((key, value)):
            pairs.append((ref.at[rows - EARLY :, here], tops.at[i, :, here]))
        for i, ref in enumerate((gate, gate_long, key_long)):
            pairs.append((ref.at[rows - RIM :, here], ends.at[i, :, here]))
        copies.append(
            [
                pltpu.make_async_copy(source, target, arrived.at[chunk, i])
                for i, (source, target) in enumerate(pairs)
            ]
        )
    for group in copies:
        for copy in group:
            copy.start()
    for chunk in range(width // WIDTH):
        here = pl.ds(chunk * WIDTH, WIDTH)
        for copy in copies[chunk]:
            copy.wait()
        for lanes in lane_tiles(chunk * WIDTH):
            key_part, value_part = tops[0, :, lanes].astype(F32), tops[1, :, lanes].astype(F32)
            product = ahead_filter(key_part, taps[0, :, lanes]) * ahead_filter(
                value_part, taps[1, :, lanes]
            )
            row = rows_of((TILE, LANES))
            gate_end, gate_long_end, key_long_end = (
                ends[i, :, lanes].astype(F32)[TILE:] for i in range(3)
            )
            first = jnp.where(
                row < 2,
                pltpu.roll(key_part[-TILE:], 2, 0),
                jnp.where(row < 4, pltpu.roll(value_part[-TILE:], 4, 0), gate_end),
            )
            second = jnp.where(
                row < 2,
                pltpu.roll(gate_long_end, 2, 0),
                jnp.where(row < 4, pltpu.roll(key_long_end, 4, 0), product[TILE:RIM]),
            )
            out[:, lanes] = jnp.concatenate([first, second, product[RIM:]], 0).astype(BF16)


def mode_tables(rates, mode, lanes, offset, sign):
    rate = jnp.broadcast_to(rates[mode : mode + 1, lanes], (TILE, LANES))
    row = rows_of((TILE, LANES)).astype(F32)
    return jnp.exp(-rate * (offset + sign * row)), jnp.exp(-TILE * rate)


def response(starts, steps, count, emit):
    parts = list(starts)
    for i in range(count):
        level = parts
        while len(level) > 1:
            level = [a + b for a, b in zip(level[::2], level[1::2])]
        emit(i, level[0])
        if i + 1 < count:
            parts = [part * step for part, step in zip(parts, steps)]


def lane_tiles(base):
    starts = [base + tile * LANES for tile in range(WIDTH // LANES)]
    if isinstance(base, int):
        return [pl.ds(start, LANES) for start in starts]
    return [pl.ds(pl.multiple_of(start, LANES), LANES) for start in starts]


def impulse_kernel(
    count, place, rates, weights, exact_rows, _, long_hat, carry, leads, decays, tails, impulse
):
    modes, width = rates.shape
    rows = impulse.shape[0]
    for i, weight in enumerate(carry_weights(place[0], count, rows, rates[...])):
        carry[i] = weight

    def step(here, base):
        for tile, lanes in enumerate(lane_tiles(base)):
            starts, steps = [], []
            for mode in range(modes):
                lead, decay = mode_tables(rates, mode, lanes, 0.0, 1.0)
                start = lead * weights[mode : mode + 1, lanes]
                leads[mode, :, lanes] = start * jnp.exp(-rates[mode : mode + 1, lanes])
                decays[mode, :, lanes] = decay
                tails[mode, :, lanes] = mode_tables(rates, mode, lanes, TILE - 1.0, -1.0)[0]
                starts.append(start)
                steps.append(decay)

            def emit(i, total):
                impulse[i * TILE : (i + 1) * TILE, tile * LANES : (tile + 1) * LANES] = total

            response(starts, steps, rows // TILE, emit)
        for block in range(rows // BLOCK):
            long_hat[block, :, here] = forward_exact(
                exact_rows[...], impulse[block * BLOCK : (block + 1) * BLOCK].astype(BF16)
            )
        for block in reversed(range(1, rows // BLOCK)):
            long_hat[block, :, here] = long_hat[block, :, here] + turned(
                long_hat[block - 1, :, here]
            )

    over_channels(width, step)


def own_kernel(
    gate, key, value, short, skip, taps, split_rows, exact_rows, backward, _,
    conv_early, gate_early, mixed_late, squares_late, taps_hat, heads, sums,
):
    rows, width = gate.shape
    sums[...] = jnp.zeros(sums.shape, F32)

    def step(here, base):
        hat = forward_split(split_rows[...], taps[:, here])
        taps_hat[:, here] = hat
        keys, values, gates = (ref[:, here].astype(F32) for ref in (key, value, gate))
        heads[:, here] = jnp.concatenate(
            [part[:TILE] for part in (keys, values, gates)]
            + [taps[BLOCK - TILE :, here]],
            0,
        )
        product = shifted_filter(keys, short[1, :, here]) * shifted_filter(
            values, short[2, :, here]
        )
        row = rows_of((TILE, WIDTH))
        product = jnp.concatenate(
            [jnp.where(row < 2, 0.0, product[:TILE]), product[TILE:]], 0
        ).astype(BF16)
        before = None
        conv = []
        for block in range(rows // BLOCK):
            now = forward_exact(exact_rows[...], product[block * BLOCK : (block + 1) * BLOCK])
            window = now if before is None else now + turned(before)
            conv.append(backward_exact(backward[...], times(hat, window)))
            before = now
        total = jnp.concatenate(conv, 0) + skip[:, here] * product.astype(F32)
        feat = shifted_filter(gates, short[0, :, here])
        conv_early[:, here] = total[:EARLY]
        gate_early[:, here] = feat[:EARLY]
        mixed = (feat[EARLY:] * total[EARLY:]).astype(BF16)
        mixed_late[:, here] = mixed
        kept = mixed.astype(F32)
        sums[...] = sums[...] + lane_parts(kept * kept)

    over_channels(width, step)
    squares_late[...] = row_sums(sums[...])


def medium_kernel(
    halo, heads, short, skip, taps_hat, exact_rows, backward,
    conv_early, gate_early, mixed_late, _, __,
    mixed, mixed_rim, squares, rim_long, total,
):
    width = halo.shape[1]
    total[...] = jnp.zeros(total.shape, F32)

    def step(here, base):
        halo_part = halo[:, here].astype(F32)
        rim, rim_late = halo_part[:TILE], halo_part[TILE:RIM]
        rim_long[:, here] = rim_late
        row = rows_of((TILE, WIDTH))
        key_part, value_part, gate_part, tail = (
            heads[i * TILE : (i + 1) * TILE, here] for i in range(4)
        )
        keys = jnp.where(row >= 6, pltpu.roll(key_part, 6, 0), pltpu.roll(rim, 4, 0))
        values = jnp.where(row >= 6, pltpu.roll(value_part, 6, 0), pltpu.roll(rim, 2, 0))
        start = shifted_filter(keys, short[1, :, here]) * shifted_filter(values, short[2, :, here])
        start = start.astype(BF16).astype(F32)
        end = jnp.where(row >= 6, start, halo_part[-TILE:])
        window = jnp.concatenate([halo_part[RIM:-TILE], end], 0).astype(BF16)
        spectrum = times(taps_hat[:, here], forward_exact(exact_rows[...], window))
        late = dot(backward[...], spectrum.astype(BF16))
        tap_a, tap_b, tap_c = (tail[i : i + 1] for i in (7, 6, 5))
        far_a, far_b, far_c = (rim_late[i : i + 1] for i in (5, 6, 7))
        skip_part = skip[:, here]
        rim_conv = late[TILE:RIM] + skip_part * pltpu.roll(end, 2, 0)
        rim_conv = rim_conv + jnp.where(
            row == 6, tap_a * far_a + tap_b * far_b + tap_c * far_c, tap_a * far_b + tap_b * far_c
        )
        rim_conv = jnp.where(row >= 6, rim_conv, 0.0)
        early = conv_early[:, here] + late[RIM:]
        extra = skip_part * jnp.where(row < 2, pltpu.roll(start, 2, 0), 0.0)
        extra = extra + jnp.where(row == 0, tap_a * far_c, 0.0)
        gates = shifted_filter(jnp.concatenate([rim, gate_part], 0), short[0, :, here])
        conv = jnp.concatenate([rim_conv, early[:TILE] + extra, early[TILE:]], 0)
        feat = jnp.concatenate([gates, gate_early[TILE:, here]], 0)
        kept = (feat * conv).astype(BF16).astype(F32)
        mixed[:EARLY, here] = kept[TILE:].astype(BF16)
        mixed[EARLY:, here] = mixed_late[:, here]
        mixed_rim[:, here] = kept[:TILE]
        total[...] = total[...] + lane_parts(kept * kept)

    over_channels(width, step, unrolled=True)
    squares[...] = row_sums(total[...])


def late_kernel(
    all_width, squares, mixed_late, key_long, gain, short, decays, tails,
    product_out, state, late_factors,
):
    rows, width = key_long.shape
    modes = decays.shape[0]
    factors = norm_factors(squares[...], all_width)
    late_factors[...] = factors

    def step(here, base):
        for lanes in lane_tiles(base):
            frame = mixed_late[:, lanes].astype(F32) * factors
            feat = shifted_filter(frame, short[2, :, lanes] * gain[:, lanes])
            keys = shifted_filter(key_long[EARLY:, lanes].astype(F32), short[1, :, lanes])
            product = (keys * feat)[TURN - EARLY :]
            product_out[:, lanes] = product.astype(BF16)
            held = [product[:TILE]] * modes
            steps = [decays[mode, :, lanes] for mode in range(modes)]
            for i in range(TILE, rows - TURN, TILE):
                held = [old * decay + product[i : i + TILE] for old, decay in zip(held, steps)]
            for mode in range(modes):
                state[mode : mode + 1, lanes] = sublane_sum(held[mode] * tails[mode, :, lanes])

    over_channels(width, step, unrolled=True)


def value_kernel(
    mixed, mixed_rim, gain, key_long, gate_long, rim_long, short, rates, tails,
    parts, tails_far, gate_feat,
):
    rows, width = mixed.shape
    modes = rates.shape[0]

    def step(here, base):
        frame = jnp.concatenate([mixed_rim[:, here], mixed[:TURN, here].astype(F32)], 0)
        keys = shifted_filter(
            jnp.concatenate(
                [pltpu.roll(rim_long[:, here], 4, 0), key_long[:TURN, here].astype(F32)], 0
            ),
            short[1, :, here],
        )[TILE:]
        gates = jnp.concatenate(
            [pltpu.roll(rim_long[:, here], 6, 0), gate_long[:, here].astype(F32)], 0
        )
        gate_feat[:, here] = shifted_filter(gates, short[0, :, here])[TILE:]
        weights = short[2, :, here] * gain[:, here]
        for j in range(3):
            moved = frame if j == 0 else pltpu.roll(frame, j, 0)
            parts[j, :, here] = keys * (weights[j : j + 1] * moved[TILE:])
        for mode in range(modes):
            tails_far[mode, :, here] = tails[mode, :, here] * jnp.exp(
                (TURN - rows) * rates[mode : mode + 1, here]
            )

    over_channels(width, step, unrolled=True)


def state_kernel(
    all_width, squares, late_factors, parts, tails_far, decays, state_late,
    product_out, state, factors,
):
    width = product_out.shape[1]
    modes = decays.shape[0]
    inverse = norm_factors(squares[...], all_width)
    inverse = jnp.concatenate(
        [inverse, late_factors[: TURN - EARLY]], 0
    )
    factors[0] = inverse[TILE:]
    factors[1] = pltpu.roll(inverse, 1, 0)[TILE:]
    factors[2] = pltpu.roll(inverse, 2, 0)[TILE:]

    def step(here, base):
        for lanes in lane_tiles(base):
            steps = [decays[mode, :, lanes] for mode in range(modes)]
            held = None
            for i in range(0, TURN, 2 * TILE):
                part = slice(i, i + 2 * TILE)
                product = (
                    parts[0, part, lanes] * factors[0, part]
                    + parts[1, part, lanes] * factors[1, part]
                    + parts[2, part, lanes] * factors[2, part]
                )
                product_out[part, lanes] = product.astype(BF16)
                for piece in (product[:TILE], product[TILE:]):
                    if held is None:
                        held = [piece] * modes
                    else:
                        held = [old * decay + piece for old, decay in zip(held, steps)]
            for mode in range(modes):
                state[mode : mode + 1, lanes] = state_late[mode : mode + 1, lanes] + sublane_sum(
                    held[mode] * tails_far[mode, :, lanes]
                )

    over_channels(width, step, unrolled=True)


def local_kernel(early, late, long_hat, skip, exact_rows, backward, out, done):
    rows, width = out.shape
    done[...] = jnp.zeros(done.shape, F32)

    def step(here, base):
        spectra = []
        product = jnp.concatenate([early[:, here].astype(F32), late[:, here].astype(F32)], 0)
        for block in range(rows // BLOCK):
            part = slice(block * BLOCK, (block + 1) * BLOCK)
            piece = product[part]
            spectra.append(forward_exact(exact_rows[...], piece.astype(BF16)))
            total = times(long_hat[0, :, here], spectra[block])
            for lag in range(1, block + 1):
                total = total + times(long_hat[lag, :, here], spectra[block - lag])
            out[part, here] = backward_exact(backward[...], total) + skip[:, here] * piece

    over_channels(width, step, unrolled=True)


def modal_tables(state, decays, leads, lanes):
    modes = decays.shape[0]
    starts = [leads[mode, :, lanes] * state[mode : mode + 1, lanes] for mode in range(modes)]
    return starts, [decays[mode, :, lanes] for mode in range(modes)]


def near_kernel(
    state, decays, leads, local, gate_feat, mixed, _,
    near, mixed_out, out, held_out, sent,
):
    rows, width = local.shape
    copies = [pltpu.make_async_copy(mixed, mixed_out, sent.at[width // WIDTH])]
    copies[0].start()

    def step(here, base):
        for lanes in lane_tiles(base):

            held = []

            def emit(i, total):
                part = slice(i * TILE, (i + 1) * TILE)
                held.append(gate_feat[part, lanes] * (local[part, lanes] + total))
                near[part, lanes] = held[-1]
                if i % 2 == 1:
                    held_out[(i - 1) * TILE : (i + 1) * TILE, lanes] = jnp.concatenate(
                        held[-2:], 0
                    ).astype(BF16)

            response(*modal_tables(state, decays, leads, lanes), rows // TILE, emit)
        copy = pltpu.make_async_copy(
            held_out.at[:, here], out.at[:, here], sent.at[base // WIDTH]
        )
        copy.start()
        copies.append(copy)

    over_channels(width, step, unrolled=True)
    for copy in copies:
        copy.wait()


def finish_kernel(count, place, state, decays, leads, near, gate_feat, _, out, held_out, sent):
    rows, width = near.shape
    group, radix = list(stages(count))[-1] if count > 1 else (1, 1)

    @pl.when((place[0] // group) % radix > 0)
    def _():
        copies = []
        for chunk in range(width // PART):
            here = pl.ds(chunk * PART, PART)
            for tile in range(PART // LANES):
                lanes = slice(chunk * PART + tile * LANES, chunk * PART + (tile + 1) * LANES)
                held = []

                def emit(i, total):
                    part = slice(i * TILE, (i + 1) * TILE)
                    held.append(near[part, lanes] + gate_feat[part, lanes] * total)
                    if i % 2 == 1:
                        held_out[(i - 1) * TILE : (i + 1) * TILE, lanes] = jnp.concatenate(
                            held[-2:], 0
                        ).astype(BF16)

                response(*modal_tables(state, decays, leads, lanes), rows // TILE, emit)
            copy = pltpu.make_async_copy(held_out.at[:, here], out.at[:, here], sent.at[chunk])
            copy.start()
            copies.append(copy)
        for copy in copies:
            copy.wait()


SCALAR = pl.BlockSpec(memory_space=pltpu.SMEM)
KEPT = pl.BlockSpec(memory_space=pltpu.VMEM)
FAR = pl.BlockSpec(memory_space=pl.ANY)
MIB = 1024 * 1024


def call(kernel, name, in_specs, out_shape, scratch=(), flops=0, moved=0, room=12, out_specs=None, aliases=None):
    return pl.pallas_call(
        kernel,
        in_specs=in_specs,
        out_specs=out_specs or jax.tree.map(lambda _: KEPT, out_shape),
        out_shape=out_shape,
        scratch_shapes=list(scratch),
        input_output_aliases=aliases or {},
        compiler_params=pltpu.CompilerParams(vmem_limit_bytes=room * MIB),
        name=name,
        cost_estimate=pl.CostEstimate(flops=flops, bytes_accessed=moved, transcendentals=0),
    )


def in_hbm(value):
    return pltpu.with_memory_space_constraint(value, pltpu.HBM)


def arr(shape, dtype):
    return jax.ShapeDtypeStruct(shape, dtype)


def passed_along(value, axis, steps):
    count = lax.axis_size(axis)
    return lax.ppermute(value, axis, [(source, source + steps) for source in range(count - steps)])


def exchanged(value, axis, flip):
    count = lax.axis_size(axis)
    return lax.ppermute(value, axis, [(source, source ^ flip) for source in range(count)])


def sum_over(value, axis):
    total = value
    for part in [exchanged(value, axis, turn) for turn in range(1, lax.axis_size(axis))]:
        total = total + part
    return total


def stages(count):
    group = 1
    while group < count:
        radix = 4 if count // group >= 4 else 2
        yield group, radix
        group *= radix


def carry_weights(place, count, row_count, rates):
    for group, radix in stages(count):
        digit = (place // group) % radix
        within = (place % group).astype(F32)
        for turn in range(radix):
            member = digit ^ turn
            behind = (digit - 1 - member).astype(F32) * group + within
            decay = jnp.exp(-rates * (row_count * jnp.maximum(behind, 0.0)))
            yield jnp.where(member < digit, decay, 0.0)
            left = ((radix - 1 - member) * group).astype(F32)
            yield jnp.exp(-rates * (row_count * left))


def carried_state(state, weights, beside):
    count = lax.axis_size("ctx")
    known = incoming = jnp.zeros_like(state)
    sent = state
    at = 0
    for group, radix in stages(count):
        known = known + incoming
        if group > 1 and group * radix == count:
            state = state + beside
        sent = state.astype(BF16)
        got = [state]
        for turn in range(1, radix):
            got.append(exchanged(sent, "ctx", turn * group).astype(F32))
        incoming = sum(weights[at + 2 * turn] * got[turn] for turn in range(radix))
        state = sum(weights[at + 2 * turn + 1] * got[turn] for turn in range(radix))
        at += 2 * radix
    return known, incoming, sent


def body(
    gate_medium,
    key_medium,
    value_medium,
    short_medium,
    filter_medium,
    skip_medium,
    norm_gain,
    gate_long,
    key_long,
    short_long,
    decay_rates,
    residues,
    skip_long,
):
    rows, width = gate_medium.shape
    modes = decay_rates.shape[0]
    blocks = rows // BLOCK
    count = lax.axis_size("ctx")
    all_width = width * lax.axis_size("ch")
    exact_rows, split_rows, backward, backward_late = (jnp.asarray(m) for m in transforms())
    far = [
        in_hbm(value)
        for value in (key_medium, value_medium, gate_medium, gate_long, key_long, short_medium)
    ]
    place = lax.axis_index("ctx").astype(jnp.int32).reshape(1)
    pack = call(
        pack_kernel, "pack", [SCALAR] + [FAR] * 6, arr((EARLY, width), BF16),
        [
            pltpu.VMEM((2, EARLY, width), BF16), pltpu.VMEM((3, RIM, width), BF16),
            pltpu.VMEM((2, 3, width), F32), pltpu.SemaphoreType.DMA((width // WIDTH, 6)),
        ],
    )(place, *far)
    halo = passed_along(pack, "ctx", 1)

    skip_row = skip_medium[None]
    mode_weight = residues * jnp.sqrt(-jnp.expm1(-2.0 * decay_rates))
    turns = sum(2 * radix for _, radix in stages(count)) or 1
    conv_early, gate_early, mixed_late, squares_late, taps_hat, heads = call(
        own_kernel, "own", [KEPT] * 10,
        [
            arr((EARLY, width), F32), arr((EARLY, width), F32),
            arr((rows - EARLY, width), BF16), arr((TILE, rows - EARLY), F32),
            arr((2 * BLOCK, width), F32), arr((4 * TILE, width), F32),
        ],
        [pltpu.VMEM((rows - EARLY, LANES), F32)],
        flops=2000 * rows * width, moved=10 * rows * width, room=16,
    )(
        gate_medium, key_medium, value_medium, short_medium, skip_row, filter_medium, split_rows,
        exact_rows, backward, pack,
    )

    table = arr((modes, TILE, width), F32)
    long_hat, carry, leads, decays, tails = call(
        lambda *refs: impulse_kernel(count, *refs), "impulse",
        [SCALAR] + [KEPT] * 4,
        [
            arr((blocks, 2 * BLOCK, width), F32), arr((turns, modes, width), F32),
            table, table, table,
        ],
        [pltpu.VMEM((rows, WIDTH), F32)],
        flops=2000 * rows * width, moved=10 * rows * width,
    )(place, decay_rates, mode_weight, exact_rows, squares_late)

    total_late = sum_over(squares_late, "ch")
    product_late, state_late, late_factors = call(
        lambda *refs: late_kernel(all_width, *refs), "late", [KEPT] * 7,
        [
            arr((rows - TURN, width), BF16), arr((modes, width), F32),
            arr((rows - EARLY, LANES), F32),
        ],
        flops=100 * rows * width, moved=10 * rows * width,
    )(total_late, mixed_late, key_long, norm_gain[None], short_long, decays, tails)

    mixed_medium, mixed_rim, squares, rim_long = call(
        medium_kernel, "medium", [KEPT] * 12,
        [
            arr((rows, width), BF16), arr((TILE, width), F32), arr((TILE, EARLY + TILE), F32),
            arr((TILE, width), F32),
        ],
        [pltpu.VMEM((EARLY + TILE, LANES), F32)],
        flops=1000 * rows * width, moved=10 * rows * width,
    )(
        halo, heads, short_medium, skip_row, taps_hat, exact_rows, backward_late,
        conv_early, gate_early, mixed_late, state_late, carry,
    )

    total_squares = sum_over(squares, "ch")
    long_parts, tails_far, gate_feat = call(
        value_kernel, "value", [KEPT] * 9,
        [arr((3, TURN, width), F32), table, arr((rows, width), F32)],
        flops=1000 * rows * width, moved=10 * rows * width,
    )(
        mixed_medium, mixed_rim, norm_gain[None], key_long, gate_long, rim_long, short_long,
        decay_rates, tails,
    )
    product_early, state = call(
        lambda *refs: state_kernel(all_width, *refs), "state", [KEPT] * 6,
        [arr((TURN, width), BF16), arr((modes, width), F32)],
        [pltpu.VMEM((3, TURN, LANES), F32)],
        flops=100 * rows * width, moved=10 * rows * width,
    )(total_squares, late_factors, long_parts, tails_far, decays, state_late)

    local, done = call(
        local_kernel, "local", [KEPT] * 6, [arr((rows, width), F32), arr((1, width), F32)],
        flops=2000 * rows * width, moved=14 * rows * width,
    )(product_early, product_late, long_hat, skip_long[None], exact_rows, backward)
    known, incoming, last_sent = carried_state(state, carry, done)
    near, mixed_out, mixed_long = call(
        near_kernel, "near", [KEPT] * 7,
        [
            arr((rows, width), F32), arr((rows, width), BF16), arr((rows, width), BF16),
        ],
        [pltpu.VMEM((rows, width), BF16), pltpu.SemaphoreType.DMA((width // WIDTH + 1,))],
        out_specs=[KEPT, FAR, FAR],
        flops=1000 * rows * width, moved=14 * rows * width,
    )(known, decays, leads, local, gate_feat, mixed_medium, last_sent)
    mixed_long = call(
        lambda *refs: finish_kernel(count, *refs), "finish", [SCALAR] + [KEPT] * 5 + [FAR],
        arr((rows, width), BF16),
        [pltpu.VMEM((rows, width), BF16), pltpu.SemaphoreType.DMA((width // PART,))],
        out_specs=FAR, aliases={6: 0},
        flops=100 * rows * width, moved=8 * rows * width,
    )(place, incoming, decays, leads, near, gate_feat, mixed_long)
    return (mixed_out, mixed_long)


def solution(mesh):
    placed = (
        P("ctx", "ch"),
        P("ctx", "ch"),
        P("ctx", "ch"),
        P(None, None, "ch"),
        P(None, "ch"),
        P("ch"),
        P("ch"),
        P("ctx", "ch"),
        P("ctx", "ch"),
        P(None, None, "ch"),
        P(None, "ch"),
        P(None, "ch"),
        P("ch"),
    )
    return jax.shard_map(
        body,
        mesh=mesh,
        in_specs=placed,
        out_specs=(P("ctx", "ch"), P("ctx", "ch")),
        check_vma=False,
    )
```
